32 devices in a mesh: ctx: 8 (over y, x, core), head: 4 (over z).
Axes of the slice: x: 2, y: 2, z: 4, core: 2. Of those that a mesh axis runs over, the one named last changes fastest.
Arguments:
- queries: bfloat16 [2048, 4096], P('ctx', 'head'), may hold values from -80 to 80
- keys: bfloat16 [2048, 2048], P('ctx', 'head'), may hold values from -6 to 6
- values: bfloat16 [2048, 2048], P('ctx', 'head'), may hold values from -6 to 6
- grad_out: bfloat16 [2048, 4096], P('ctx', 'head'), may hold values from -6 to 6
- chosen: int32 [32, 16, 16], P('ctx', 'head'), may hold values from 0 to 31, as said below
- w_query: bfloat16 [4608, 4096], P(None, 'head'), may hold values from -0.09375 to 0.09375
- w_key: bfloat16 [4608, 2048], P(None, 'head'), may hold values from -0.09375 to 0.09375
- w_value: bfloat16 [4608, 2048], P(None, 'head'), may hold values from -0.09375 to 0.09375
Outputs:
- grad_queries: bfloat16 [2048, 4096], P('ctx', 'head')
- grad_keys: bfloat16 [2048, 2048], P('ctx', 'head')
- grad_values: bfloat16 [2048, 2048], P('ctx', 'head')
- grad_input: bfloat16 [2048, 4608], P('ctx', 'head')
The draws below stay inside these ranges and needn't reach their ends.
Inputs may be any that keep to these rules, and one draw needn't show every extreme that they name: `chosen`: each list names 16 different blocks; it always names block 0 and the query's own block, and a query block b below 16 names every block 0 .. b; entries above the query's own block contribute no keys.
All inputs are finite; a program needn't handle non-finite values.
Results may differ from the reference program's by a relative error of at most 0.019.
Values may be sent and summed in bfloat16 or wider, within the bound.
No kernel may reach another device: no remote copies, remote signals or barrier semaphores. Data moves between devices by JAX's collectives and lax.ppermute only.
A program may use at most 128 MiB of HBM per device.

```python
import math
import jax
import jax.numpy as jnp
from jax import lax

D = 4608
HEADS = 32
GROUPS = 16
HEAD_DIM = 128
BLOCK = 64
TOPK = 16
TOK_DEV = 256
TOKENS = 2048
NBLK = 32
N_CTX = 8
N_HEAD = 4


def joint_fields(key):
    base_key = jax.random.fold_in(key, 11)
    k_keys = jax.random.fold_in(base_key, 0)
    k_query = jax.random.fold_in(base_key, 3)
    key_field = jax.random.truncated_normal(k_keys, -6.0, 6.0, (TOKENS, GROUPS * HEAD_DIM), jnp.float32)
    query_field = jax.random.truncated_normal(k_query, -6.0, 6.0, (TOKENS, HEADS * HEAD_DIM), jnp.float32)
    return (query_field, key_field)


def draw_queries(key, part):
    return joint_fields(key)[0].astype(jnp.bfloat16)


def draw_keys(key, part):
    return joint_fields(key)[1].astype(jnp.bfloat16)


def draw_chosen(key, part):
    count = TOKENS // BLOCK
    raw_scores = jax.random.randint(jax.random.fold_in(key, 23), (count, GROUPS, count), 0, 65536, dtype=jnp.int32)
    column = jnp.arange(count, dtype=jnp.int32)[None, None, :]
    own_block = jnp.arange(count, dtype=jnp.int32)[:, None, None]
    ranking = raw_scores * count + column
    ranking = ranking + jnp.where(column <= own_block, 2 ** 27, 0)
    ranking = ranking + jnp.where((column == 0) | (column == own_block), 2 ** 28, 0)
    ignored, picked = lax.top_k(ranking, TOPK)
    return picked.astype(jnp.int32)


def steps_of(key, dims, cuts, least, high):
    def one(dim, shards_of):
        steps = jax.random.uniform(jax.random.fold_in(jax.random.fold_in(key, 6), dim), (shards_of,), jnp.float32, least / len(cuts), high / len(cuts))
        return jnp.repeat(jnp.exp(steps), dims[dim] // shards_of).reshape((-1,) + (1,) * (len(dims) - dim - 1))

    gain = one(*cuts[0])
    for cut in cuts[1:]:
        gain = gain * one(*cut)
    return gain


def normal_values(stream_key, dims, spread, most, pieces=(), held_as=jnp.bfloat16):
    loudness = steps_of(stream_key, dims, pieces, -0.22, 0.18) if pieces else 1.0
    drawn = jax.random.normal(stream_key, dims, jnp.float32) * spread * loudness
    return jnp.minimum(jnp.maximum(drawn, -most), most).astype(held_as)


def setup_inputs(seed: int = 0) -> dict:
    streams_of = jax.random.split(jax.random.key(seed), 9)
    queries = draw_queries(jax.random.fold_in(streams_of[8], 71), 0)
    keys = draw_keys(jax.random.fold_in(streams_of[8], 71), 0)
    values = normal_values(streams_of[2], (TOKENS, GROUPS * HEAD_DIM), 1.0, 6.0, ((0, 8), (1, 4)))
    grad_out = normal_values(streams_of[3], (TOKENS, HEADS * HEAD_DIM), 1.0, 6.0, ((0, 8), (1, 4)))
    chosen = draw_chosen(jax.random.fold_in(streams_of[8], 71), 0)
    w_query = normal_values(streams_of[5], (D, HEADS * HEAD_DIM), D ** -0.5, 0.09375, ((1, 4),))
    w_key = normal_values(streams_of[6], (D, GROUPS * HEAD_DIM), D ** -0.5, 0.09375, ((1, 4),))
    w_value = normal_values(streams_of[7], (D, GROUPS * HEAD_DIM), D ** -0.5, 0.09375, ((1, 4),))
    return dict(queries=queries, keys=keys, values=values, grad_out=grad_out, chosen=chosen, w_query=w_query, w_key=w_key, w_value=w_value)


def block_grads(key_blocks, value_blocks, query_block, grad_block, picked, first_row):
    block_len = query_block.shape[0]
    head_dim = key_blocks.shape[2]
    heads_per = query_block.shape[1] // head_dim
    scaling = 1.0 / math.sqrt(head_dim)
    key_rows = (picked[:, None] * block_len + jnp.arange(block_len, dtype=jnp.int32)[None, :]).reshape(-1).astype(jnp.int32)
    chosen_keys = jnp.take(key_blocks, picked, axis=0).reshape(-1, head_dim)
    chosen_values = jnp.take(value_blocks, picked, axis=0).reshape(-1, head_dim)
    query_rows = query_block.reshape(block_len * heads_per, head_dim)
    grad_rows = grad_block.reshape(block_len * heads_per, head_dim)
    positions = first_row + jnp.repeat(jnp.arange(block_len, dtype=jnp.int32), heads_per)
    allowed = key_rows[None, :] <= positions[:, None]
    contract = (((1,), (1,)), ((), ()))
    across = (((0,), (0,)), ((), ()))
    scores = scaling * lax.dot_general(query_rows, chosen_keys, contract, preferred_element_type=jnp.float32)
    scores = jnp.where(allowed, scores, -1e+30)
    row_max = lax.optimization_barrier(jnp.max(scores, axis=1, keepdims=True))
    weights = jnp.where(allowed, jnp.exp(scores - row_max), 0.0)
    weights = weights / lax.optimization_barrier(jnp.sum(weights, axis=1, keepdims=True))
    weights_low = weights.astype(jnp.bfloat16)
    attended = jnp.dot(weights_low, chosen_values, preferred_element_type=jnp.float32)
    deltas = lax.optimization_barrier(jnp.sum(grad_rows.astype(jnp.float32) * attended, axis=1, keepdims=True))
    grad_weights = lax.dot_general(grad_rows, chosen_values, contract, preferred_element_type=jnp.float32)
    grad_scores = (weights * (grad_weights - deltas)).astype(jnp.bfloat16)
    grad_query = scaling * jnp.dot(grad_scores, chosen_keys, preferred_element_type=jnp.float32)
    grad_key = scaling * lax.dot_general(grad_scores, query_rows, across, preferred_element_type=jnp.float32)
    grad_value = lax.dot_general(weights_low, grad_rows, across, preferred_element_type=jnp.float32)
    grad_query = grad_query.astype(jnp.bfloat16).reshape(block_len, heads_per * head_dim)
    grad_key = grad_key.reshape(picked.shape[0], block_len * head_dim)
    grad_value = grad_value.reshape(picked.shape[0], block_len * head_dim)
    return (grad_query, grad_key, grad_value)

def reference(queries, keys, values, grad_out, chosen, w_query, w_key, w_value):
    heads_per = HEADS // GROUPS
    query_width = heads_per * HEAD_DIM
    blocks_here = TOK_DEV // BLOCK
    block_step = math.gcd(blocks_here, max(1, 512 // (BLOCK * heads_per)))
    turns = blocks_here // block_step
    mapped = jax.vmap(block_grads, in_axes=(None, None, 0, 0, 0, 0))

    def one_group(group_index):
        key_all = lax.dynamic_slice_in_dim(keys, (group_index * HEAD_DIM).astype(jnp.int32), HEAD_DIM, 1).reshape(NBLK, BLOCK, HEAD_DIM)
        value_all = lax.dynamic_slice_in_dim(values, (group_index * HEAD_DIM).astype(jnp.int32), HEAD_DIM, 1).reshape(NBLK, BLOCK, HEAD_DIM)
        query_part = lax.dynamic_slice_in_dim(queries, (group_index * query_width).astype(jnp.int32), query_width, 1)
        grad_part = lax.dynamic_slice_in_dim(grad_out, (group_index * query_width).astype(jnp.int32), query_width, 1)
        picked_all = lax.dynamic_index_in_dim(chosen, group_index, 1, keepdims=False)

        def one_shard(totals, shard_index):

            def update_step(running, turn_index):
                first_block = (shard_index * blocks_here + turn_index * block_step).astype(jnp.int32)
                query_set = lax.dynamic_slice_in_dim(query_part, first_block * BLOCK, block_step * BLOCK, 0).reshape(block_step, BLOCK, query_width)
                grad_set = lax.dynamic_slice_in_dim(grad_part, first_block * BLOCK, block_step * BLOCK, 0).reshape(block_step, BLOCK, query_width)
                picked_set = lax.dynamic_slice_in_dim(picked_all, first_block, block_step, 0)
                row_set = ((first_block + jnp.arange(block_step, dtype=jnp.int32)) * BLOCK).astype(jnp.int32)
                grad_q, grad_k, grad_v = mapped(key_all, value_all, query_set, grad_set, picked_set, row_set)
                flat_blocks = picked_set.reshape(-1)
                total_k = running[0].at[flat_blocks].add(grad_k.reshape(-1, BLOCK * HEAD_DIM))
                total_v = running[1].at[flat_blocks].add(grad_v.reshape(-1, BLOCK * HEAD_DIM))
                return ((total_k, total_v), grad_q.reshape(block_step * BLOCK, query_width))
            zeros_acc = jnp.zeros((NBLK, BLOCK * HEAD_DIM), jnp.float32)
            (shard_k, shard_v), grad_q = lax.scan(update_step, (zeros_acc, zeros_acc), jnp.arange(turns, dtype=jnp.int32))
            rounded_k = lax.optimization_barrier(shard_k.astype(jnp.bfloat16)).astype(jnp.float32)
            rounded_v = lax.optimization_barrier(shard_v.astype(jnp.bfloat16)).astype(jnp.float32)
            return ((totals[0] + rounded_k, totals[1] + rounded_v), grad_q.reshape(TOK_DEV, query_width))
        zeros_sum = jnp.zeros((NBLK, BLOCK * HEAD_DIM), jnp.float32)
        (total_k, total_v), grad_q = lax.scan(one_shard, (zeros_sum, zeros_sum), jnp.arange(N_CTX, dtype=jnp.int32))
        return (grad_q.reshape(TOKENS, query_width), total_k.reshape(TOKENS, HEAD_DIM).astype(jnp.bfloat16), total_v.reshape(TOKENS, HEAD_DIM).astype(jnp.bfloat16))
    grad_q_all, grad_k_all, grad_v_all = lax.map(one_group, jnp.arange(GROUPS, dtype=jnp.int32))
    grad_queries = jnp.transpose(grad_q_all, (1, 0, 2)).reshape(TOKENS, HEADS * HEAD_DIM)
    grad_keys = jnp.transpose(grad_k_all, (1, 0, 2)).reshape(TOKENS, GROUPS * HEAD_DIM)
    grad_values = jnp.transpose(grad_v_all, (1, 0, 2)).reshape(TOKENS, GROUPS * HEAD_DIM)
    contract = (((1,), (1,)), ((), ()))
    heads_shard = HEADS // N_HEAD * HEAD_DIM
    groups_shard = GROUPS // N_HEAD * HEAD_DIM
    total_input = jnp.zeros((TOKENS, D), jnp.float32)
    for shard_index in range(N_HEAD):
        query_cols = slice(shard_index * heads_shard, (shard_index + 1) * heads_shard)
        group_cols = slice(shard_index * groups_shard, (shard_index + 1) * groups_shard)
        partial_term = lax.dot_general(grad_queries[:, query_cols], w_query[:, query_cols], contract, preferred_element_type=jnp.float32)
        partial_term = partial_term + lax.dot_general(grad_keys[:, group_cols], w_key[:, group_cols], contract, preferred_element_type=jnp.float32)
        partial_term = partial_term + lax.dot_general(grad_values[:, group_cols], w_value[:, group_cols], contract, preferred_element_type=jnp.float32)
        total_input = total_input + lax.optimization_barrier(partial_term.astype(jnp.bfloat16)).astype(jnp.float32)
    return (grad_queries, grad_keys, grad_values, total_input.astype(jnp.bfloat16))
```

```python
import functools
import math

import jax
import jax.numpy as jnp
from jax import lax
from jax.experimental import pallas as pl
from jax.experimental.pallas import tpu as pltpu
from jax.sharding import PartitionSpec as P

HEAD_DIM = 128
BLOCK = 64
LOG2E = math.log2(math.e)


def attention_kernel(n_ctx, topk, first_group, groups_here, chosen, place, *refs):
    pieces = refs[:n_ctx]
    q_ref, g_ref = refs[n_ctx : n_ctx + 2]
    dq_ref, keep_ref, send_ref = refs[n_ctx + 2 : n_ctx + 5]
    kv, acc, near, scores, packed = refs[n_ctx + 5 :]
    rows = q_ref.shape[0]
    wide = 2 * HEAD_DIM
    heads_per = q_ref.shape[1] // HEAD_DIM
    lanes = heads_per * BLOCK
    me = place[0]
    group = first_group + pl.program_id(0)
    scaling = 1.0 / math.sqrt(HEAD_DIM)
    step = scaling * LOG2E

    for k in range(n_ctx):
        kv[pl.ds(pl.multiple_of((me ^ k) * rows, rows), rows), :] = pieces[k][...]
    acc[...] = jnp.zeros_like(acc)
    offset = lax.broadcasted_iota(jnp.int32, (BLOCK, lanes), 0) - (
        lax.broadcasted_iota(jnp.int32, (BLOCK, lanes), 1) % BLOCK
    )
    blank = jnp.zeros((lanes, HEAD_DIM), jnp.bfloat16)

    def one_block(b, carry):
        own = me * (rows // BLOCK) + b
        base = (b * groups_here + group) * topk
        start = pl.multiple_of(b * BLOCK, BLOCK)
        picks = [chosen[base + i] for i in range(topk)]
        for i in range(topk):
            near[i * BLOCK : (i + 1) * BLOCK, :] = kv[
                pl.ds(pl.multiple_of(picks[i] * BLOCK, BLOCK), BLOCK), :
            ]
        q_rows = jnp.concatenate(
            [q_ref[pl.ds(start, BLOCK), h * HEAD_DIM : (h + 1) * HEAD_DIM] for h in range(heads_per)], axis=0
        )
        g_rows = jnp.concatenate(
            [g_ref[pl.ds(start, BLOCK), h * HEAD_DIM : (h + 1) * HEAD_DIM] for h in range(heads_per)], axis=0
        )
        both = jnp.concatenate(
            [jnp.concatenate([q_rows, blank], axis=1), jnp.concatenate([blank, g_rows], axis=1)], axis=0
        )
        scores[...] = lax.dot_general(
            near[...], both, (((1,), (1,)), ((), ())), preferred_element_type=jnp.float32
        )
        limits = [(own - picks[i]) * BLOCK for i in range(topk)]

        def masked(i):
            s = scores[i * BLOCK : (i + 1) * BLOCK, :lanes]
            return jnp.where(offset <= limits[i], s, -1e30)

        top = masked(0)
        for i in range(1, topk):
            top = jnp.maximum(top, masked(i))
        top = jnp.max(top, axis=0, keepdims=True)
        total = jnp.zeros((BLOCK, lanes), jnp.float32)
        delta = jnp.zeros((BLOCK, lanes), jnp.float32)
        for i in range(topk):
            part = slice(i * BLOCK, (i + 1) * BLOCK)
            e = jnp.exp2((masked(i) - top) * step)
            scores[part, :lanes] = e
            total = total + e
            delta = delta + e * scores[part, lanes:]
        total = 1.0 / jnp.sum(total, axis=0, keepdims=True)
        delta = jnp.sum(delta, axis=0, keepdims=True) * total
        for i in range(topk):
            part = slice(i * BLOCK, (i + 1) * BLOCK)
            w = scores[part, :lanes] * total
            packed[part, lanes:] = w.astype(jnp.bfloat16)
            packed[part, :lanes] = (w * (scores[part, lanes:] - delta)).astype(jnp.bfloat16)
        terms = jnp.dot(packed[...], both, preferred_element_type=jnp.float32)
        for i in range(topk):
            at = pl.ds(pl.multiple_of(picks[i] * BLOCK, BLOCK), BLOCK)
            acc[at, :] += terms[i * BLOCK : (i + 1) * BLOCK, :]
        dq = scaling * lax.dot_general(
            packed[:, :lanes],
            near[:, :HEAD_DIM],
            (((0,), (0,)), ((), ())),
            preferred_element_type=jnp.float32,
        )
        dq = dq.astype(jnp.bfloat16)
        for h in range(heads_per):
            dq_ref[pl.ds(start, BLOCK), h * HEAD_DIM : (h + 1) * HEAD_DIM] = dq[h * BLOCK : (h + 1) * BLOCK, :]
        return carry

    lax.fori_loop(0, rows // BLOCK, one_block, 0)

    for k in range(n_ctx // 2):
        for core, out in ((0, keep_ref), (1, send_ref)):
            at = pl.ds(pl.multiple_of((me ^ (2 * k + core)) * rows, rows), rows)
            out[k * rows : (k + 1) * rows, :HEAD_DIM] = (acc[at, :HEAD_DIM] * scaling).astype(jnp.bfloat16)
            out[k * rows : (k + 1) * rows, HEAD_DIM:] = acc[at, HEAD_DIM:].astype(jnp.bfloat16)


def attention(pieces, queries, grad_out, chosen, me, first_group, groups_here):
    n_ctx = len(pieces)
    rows = queries.shape[0]
    topk = chosen.shape[-1]
    wide = 2 * HEAD_DIM
    calls = pieces[0].shape[1] // wide
    width = queries.shape[1] // groups_here
    lanes = width // HEAD_DIM * BLOCK
    half = n_ctx // 2 * rows
    flops = calls * (rows // BLOCK) * 10 * topk * BLOCK * lanes * HEAD_DIM
    return pl.pallas_call(
        functools.partial(attention_kernel, n_ctx, topk, first_group, groups_here),
        out_shape=(
            jax.ShapeDtypeStruct((rows, calls * width), jnp.bfloat16),
            jax.ShapeDtypeStruct((half, calls * wide), jnp.bfloat16),
            jax.ShapeDtypeStruct((half, calls * wide), jnp.bfloat16),
        ),
        grid_spec=pltpu.PrefetchScalarGridSpec(
            num_scalar_prefetch=2,
            grid=(calls,),
            in_specs=[pl.BlockSpec((rows, wide), lambda j, *_: (0, j))] * n_ctx
            + [pl.BlockSpec((rows, width), lambda j, *_: (0, first_group + j))] * 2,
            out_specs=[
                pl.BlockSpec((rows, width), lambda j, *_: (0, j)),
                pl.BlockSpec((half, wide), lambda j, *_: (0, j)),
                pl.BlockSpec((half, wide), lambda j, *_: (0, j)),
            ],
            scratch_shapes=[
                pltpu.VMEM((n_ctx * rows, wide), jnp.bfloat16),
                pltpu.VMEM((n_ctx * rows, wide), jnp.float32),
                pltpu.VMEM((topk * BLOCK, wide), jnp.bfloat16),
                pltpu.VMEM((topk * BLOCK, 2 * lanes), jnp.float32),
                pltpu.VMEM((topk * BLOCK, 2 * lanes), jnp.bfloat16),
            ],
        ),
        compiler_params=pltpu.CompilerParams(vmem_limit_bytes=40 * 2**20),
        cost_estimate=pl.CostEstimate(
            flops=flops, bytes_accessed=8 * n_ctx * rows * wide * calls, transcendentals=0
        ),
        name="attention",
    )(chosen.reshape(-1), me.reshape(1), *pieces, queries, grad_out)


def projection_kernel(gq_ref, gk_ref, gv_ref, wq_ref, wk_ref, wv_ref, out_ref):
    contract = (((1,), (1,)), ((), ()))
    total = lax.dot_general(gq_ref[...], wq_ref[...], contract, preferred_element_type=jnp.float32)
    total += lax.dot_general(gk_ref[...], wk_ref[...], contract, preferred_element_type=jnp.float32)
    total += lax.dot_general(gv_ref[...], wv_ref[...], contract, preferred_element_type=jnp.float32)
    out_ref[...] = total.astype(jnp.bfloat16)


def projection(gq, gk, gv, wq, wk, wv):
    rows = gq.shape[0]
    out = wq.shape[0]
    tile = math.gcd(out, 512)
    held = lambda a: pl.BlockSpec(a.shape, lambda j: (0, 0))
    cut = lambda a: pl.BlockSpec((tile, a.shape[1]), lambda j: (j, 0))
    return pl.pallas_call(
        projection_kernel,
        out_shape=jax.ShapeDtypeStruct((rows, out), jnp.bfloat16),
        grid=(out // tile,),
        in_specs=[held(gq), held(gk), held(gv), cut(wq), cut(wk), cut(wv)],
        out_specs=pl.BlockSpec((rows, tile), lambda j: (0, j)),
        compiler_params=pltpu.CompilerParams(vmem_limit_bytes=40 * 2**20),
        name="projection",
    )(gq, gk, gv, wq, wk, wv)


def bits_of(mask):
    return [1 << i for i in range(mask.bit_length()) if mask >> i & 1]


def cuts_of(rows, count):
    edges = [rows * i // count // 16 * 16 for i in range(count)] + [rows]
    return [slice(edges[i], edges[i + 1]) for i in range(count)]


def exchange(x, axis, mask):
    n = lax.axis_size(axis)
    return lax.ppermute(x, axis, [(i, i ^ mask) for i in range(n)])


def gather_pieces(own, axis):
    n = lax.axis_size(axis)
    pieces = {0: own}
    far = sorted(range(2, n, 2), key=lambda m: (m.bit_count(), m))
    for mask in far:
        bits = bits_of(mask)
        cuts = cuts_of(own.shape[0], len(bits))
        parts = [exchange(pieces[mask ^ bit][cut], axis, bit) for bit, cut in zip(bits, cuts)]
        pieces[mask] = parts[0] if len(parts) == 1 else jnp.concatenate(parts, axis=0)
    for mask in range(0, n, 2):
        pieces[mask | 1] = exchange(pieces[mask], axis, 1)
    return [pieces[k] for k in range(n)]


def scatter_sum(keep, send, axis):
    n = lax.axis_size(axis)
    rows = keep.shape[0] // (n // 2)
    got = exchange(send, axis, 1)
    sums = {}
    for mask in range(0, n, 2):
        cut = slice(mask // 2 * rows, (mask // 2 + 1) * rows)
        sums[mask] = keep[cut].astype(jnp.float32) + got[cut].astype(jnp.float32)
    for mask in sorted(range(2, n, 2), key=lambda m: (-m.bit_count(), m)):
        bits = bits_of(mask)
        cuts = cuts_of(rows, len(bits))
        for bit, cut in zip(bits, cuts):
            part = exchange(sums[mask][cut].astype(jnp.bfloat16), axis, bit).astype(jnp.float32)
            whole = sums[mask ^ bit]
            pads = [(cut.start, rows - cut.stop), (0, 0)]
            sums[mask ^ bit] = whole + (part if part.shape == whole.shape else jnp.pad(part, pads))
    return sums[0].astype(jnp.bfloat16)


def line_scatter_sum(partial, axis):
    n = lax.axis_size(axis)
    me = lax.axis_index(axis)
    width = partial.shape[1] // n

    def chunk(d):
        return lax.dynamic_slice_in_dim(partial, jnp.clip(d, 0, n - 1) * width, width, 1).astype(jnp.float32)

    from_left = from_right = 0.0
    for t in range(1, n):
        right = (chunk(n - t + me) + from_left).astype(jnp.bfloat16)
        left = (chunk(t - n + me) + from_right).astype(jnp.bfloat16)
        from_left = lax.ppermute(right, axis, [(i, i + 1) for i in range(t)]).astype(jnp.float32)
        from_right = lax.ppermute(left, axis, [(n - 1 - i, n - 2 - i) for i in range(t)]).astype(jnp.float32)
    return (chunk(me) + from_left + from_right).astype(jnp.bfloat16)


def body(queries, keys, values, grad_out, chosen, w_query, w_key, w_value):
    groups = keys.shape[1] // HEAD_DIM
    rows = keys.shape[0]
    wide = 2 * HEAD_DIM
    me = lax.axis_index("ctx")
    pairs = jnp.concatenate(
        [keys.reshape(rows, groups, HEAD_DIM), values.reshape(rows, groups, HEAD_DIM)], axis=2
    ).reshape(rows, groups * wide)
    pieces = gather_pieces(pairs, "ctx")
    grad_queries, keep, send = attention(pieces, queries, grad_out, chosen, me, 0, groups)
    total = scatter_sum(keep, send, "ctx").reshape(rows, groups, wide)
    grad_keys = total[:, :, :HEAD_DIM].reshape(rows, groups * HEAD_DIM)
    grad_values = total[:, :, HEAD_DIM:].reshape(rows, groups * HEAD_DIM)
    partial = projection(grad_queries, grad_keys, grad_values, w_query, w_key, w_value)
    grad_input = line_scatter_sum(partial, "head")
    return (grad_queries, grad_keys, grad_values, grad_input)


def solution(mesh):
    return jax.shard_map(
        body,
        mesh=mesh,
        in_specs=(
            P("ctx", "head"),
            P("ctx", "head"),
            P("ctx", "head"),
            P("ctx", "head"),
            P("ctx", "head", None),
            P(None, "head"),
            P(None, "head"),
            P(None, "head"),
        ),
        out_specs=(P("ctx", "head"), P("ctx", "head"), P("ctx", "head"), P("ctx", "head")),
        check_vma=False,
    )
```

```python
import functools
import math

import jax
import jax.numpy as jnp
from jax import lax
from jax.experimental import pallas as pl
from jax.experimental.pallas import tpu as pltpu
from jax.sharding import PartitionSpec as P

HEAD_DIM = 128
BLOCK = 64
LOG2E = math.log2(math.e)


def attention_kernel(n_ctx, topk, first_group, groups_here, calls, chosen, place, *refs):
    pieces = refs[:n_ctx]
    q_ref, g_ref = refs[n_ctx : n_ctx + 2]
    dq_ref, keep_ref, send_ref = refs[n_ctx + 2 : n_ctx + 5]
    kv, acc, near, scores, packed, operand, arrived = refs[n_ctx + 5 :]
    rows = q_ref.shape[0]
    wide = 2 * HEAD_DIM
    width = q_ref.shape[1] // calls
    heads_per = width // HEAD_DIM
    lanes = heads_per * BLOCK
    blocks = rows // BLOCK
    me = place[0]
    scaling = 1.0 / math.sqrt(HEAD_DIM)
    step = scaling * LOG2E

    def piece_rows(k):
        return pl.ds(pl.multiple_of((me ^ k) * rows, rows), rows)

    def arrival(j, k):
        return pltpu.make_async_copy(
            pieces[k].at[:, pl.ds(j * wide, wide)], kv.at[j, piece_rows(k), :], arrived.at[j, k]
        )

    for j in range(calls):
        for k in range(n_ctx):
            arrival(j, k).start()
    acc[...] = jnp.zeros_like(acc)
    operand[...] = jnp.zeros_like(operand)
    offset = lax.broadcasted_iota(jnp.int32, (BLOCK, lanes), 0) - (
        lax.broadcasted_iota(jnp.int32, (BLOCK, lanes), 1) % BLOCK
    )

    def picks_of(j, b):
        own = me * blocks + b
        base = (b * groups_here + first_group + j) * topk
        listed = [chosen[base + i] for i in range(topk)]
        return own, [own] + [jnp.where(listed[i] == own, listed[0], listed[i]) for i in range(1, topk)]

    def tile(i):
        return slice(i * BLOCK, (i + 1) * BLOCK)

    def score_stage(j, b, slot):
        _, picks = picks_of(j, b)
        for i in range(topk):
            near[slot, tile(i), :] = kv[j, pl.ds(pl.multiple_of(picks[i] * BLOCK, BLOCK), BLOCK), :]
        for h in range(heads_per):
            at = slice(j * width + h * HEAD_DIM, j * width + (h + 1) * HEAD_DIM)
            operand[slot, tile(h), :HEAD_DIM] = q_ref[tile(b), at]
            operand[slot, lanes + h * BLOCK : lanes + (h + 1) * BLOCK, HEAD_DIM:] = g_ref[tile(b), at]
        scores[slot] = lax.dot_general(
            near[slot], operand[slot], (((1,), (1,)), ((), ())), preferred_element_type=jnp.float32
        )

    def weight_stage(j, b, slot):
        own, picks = picks_of(j, b)
        bias = [jnp.where(picks[i] > own, -1e30, 0.0) for i in range(topk)]
        first = jnp.where(offset <= 0, scores[slot, tile(0), :lanes], -1e30)
        top = first
        for i in range(1, topk):
            top = jnp.maximum(top, scores[slot, tile(i), :lanes] + bias[i])
        top = jnp.max(top, axis=0, keepdims=True)
        total = jnp.zeros((BLOCK, lanes), jnp.float32)
        delta = jnp.zeros((BLOCK, lanes), jnp.float32)
        for i in range(topk):
            s = first - top if i == 0 else scores[slot, tile(i), :lanes] - (top - bias[i])
            e = jnp.exp2(s * step)
            scores[slot, tile(i), :lanes] = e
            total = total + e
            delta = delta + e * scores[slot, tile(i), lanes:]
        total = 1.0 / jnp.sum(total, axis=0, keepdims=True)
        delta = jnp.sum(delta, axis=0, keepdims=True) * total
        for i in range(topk):
            w = scores[slot, tile(i), :lanes] * total
            packed[slot, tile(i), lanes:] = w.astype(jnp.bfloat16)
            packed[slot, tile(i), :lanes] = (w * (scores[slot, tile(i), lanes:] - delta)).astype(jnp.bfloat16)

    def term_stage(j, b, slot):
        _, picks = picks_of(j, b)
        terms = jnp.dot(packed[slot], operand[slot], preferred_element_type=jnp.float32)
        for i in range(topk):
            at = pl.ds(pl.multiple_of(picks[i] * BLOCK, BLOCK), BLOCK)
            acc[j, at, :] += terms[tile(i), :]
        dq = scaling * lax.dot_general(
            packed[slot, :, :lanes],
            near[slot, :, :HEAD_DIM],
            (((0,), (0,)), ((), ())),
            preferred_element_type=jnp.float32,
        )
        dq = dq.astype(jnp.bfloat16)
        for h in range(heads_per):
            dq_ref[tile(b), j * width + h * HEAD_DIM : j * width + (h + 1) * HEAD_DIM] = dq[tile(h), :]

    def out_stage(j):
        for k in range(n_ctx // 2):
            to = slice(k * rows, (k + 1) * rows)
            for core, out in ((0, keep_ref), (1, send_ref)):
                at = piece_rows(2 * k + core)
                cols = slice(j * wide, j * wide + HEAD_DIM)
                out[to, cols] = (acc[j, at, :HEAD_DIM] * scaling).astype(jnp.bfloat16)
                cols = slice(j * wide + HEAD_DIM, (j + 1) * wide)
                out[to, cols] = acc[j, at, HEAD_DIM:].astype(jnp.bfloat16)

    slots = near.shape[0]
    work = [(j, b) for j in range(calls) for b in range(blocks)]
    for t in range(len(work) + 2):
        if t < len(work):
            j, b = work[t]
            if b == 0:
                for k in range(n_ctx):
                    arrival(j, k).wait()
            score_stage(j, b, t % slots)
        if 1 <= t <= len(work):
            weight_stage(*work[t - 1], (t - 1) % slots)
        if t >= 2:
            term_stage(*work[t - 2], (t - 2) % slots)
            if work[t - 2][1] == blocks - 1:
                out_stage(work[t - 2][0])


def attention(pieces, queries, grad_out, chosen, me, first_group, groups_here):
    n_ctx = len(pieces)
    rows = queries.shape[0]
    topk = chosen.shape[-1]
    wide = 2 * HEAD_DIM
    calls = pieces[0].shape[1] // wide
    width = queries.shape[1] // groups_here
    lanes = width // HEAD_DIM * BLOCK
    half = n_ctx // 2 * rows
    flops = calls * (rows // BLOCK) * 10 * topk * BLOCK * lanes * HEAD_DIM
    slots = 3
    whole = lambda shape: pl.BlockSpec(shape, lambda j, *_: (0, 0))
    return pl.pallas_call(
        functools.partial(attention_kernel, n_ctx, topk, first_group, groups_here, calls),
        out_shape=(
            jax.ShapeDtypeStruct((rows, calls * width), jnp.bfloat16),
            jax.ShapeDtypeStruct((half, calls * wide), jnp.bfloat16),
            jax.ShapeDtypeStruct((half, calls * wide), jnp.bfloat16),
        ),
        grid_spec=pltpu.PrefetchScalarGridSpec(
            num_scalar_prefetch=2,
            grid=(1,),
            in_specs=[pl.BlockSpec(memory_space=pltpu.HBM)] * n_ctx
            + [pl.BlockSpec((rows, calls * width), lambda j, *_: (0, first_group // calls))] * 2,
            out_specs=[
                whole((rows, calls * width)),
                whole((half, calls * wide)),
                whole((half, calls * wide)),
            ],
            scratch_shapes=[
                pltpu.VMEM((calls, n_ctx * rows, wide), jnp.bfloat16),
                pltpu.VMEM((calls, n_ctx * rows, wide), jnp.float32),
                pltpu.VMEM((slots, topk * BLOCK, wide), jnp.bfloat16),
                pltpu.VMEM((slots, topk * BLOCK, 2 * lanes), jnp.float32),
                pltpu.VMEM((slots, topk * BLOCK, 2 * lanes), jnp.bfloat16),
                pltpu.VMEM((slots, 2 * lanes, wide), jnp.bfloat16),
                pltpu.SemaphoreType.DMA((calls, n_ctx)),
            ],
        ),
        compiler_params=pltpu.CompilerParams(vmem_limit_bytes=56 * 2**20),
        cost_estimate=pl.CostEstimate(
            flops=flops, bytes_accessed=8 * n_ctx * rows * wide * calls, transcendentals=0
        ),
        name="attention",
    )(chosen.reshape(-1), me.reshape(1), *pieces, queries, grad_out)


def projection_kernel(chunks, width, summed, order, *refs):
    gq_ref, *parts = refs[: summed + 1]
    wq_ref, wk_ref, wv_ref = refs[summed + 1 : summed + 4]
    outs = refs[summed + 4 :]
    if summed > 2:
        gk_ref, gv_ref, *outs = outs
    else:
        gk_ref, gv_ref = parts
    out_refs, (wq, wk, wv, arrived) = outs[:chunks], outs[chunks:]

    def arrivals(i):
        at = pl.ds(pl.multiple_of(order[i] * width, width), width)
        return [
            pltpu.make_async_copy(src.at[at, :], dst.at[i], arrived.at[i, k])
            for k, (src, dst) in enumerate(((wq_ref, wq), (wk_ref, wk), (wv_ref, wv)))
        ]

    for i in range(chunks):
        for copy in arrivals(i):
            copy.start()
    if summed > 2:
        groups = gk_ref.shape[1] // HEAD_DIM
        for g in range(groups):
            for side, out in ((0, gk_ref), (1, gv_ref)):
                at = slice((2 * g + side) * HEAD_DIM, (2 * g + side + 1) * HEAD_DIM)
                total = parts[0][:, at].astype(jnp.float32)
                for part in parts[1:]:
                    total += part[:, at].astype(jnp.float32)
                out[:, g * HEAD_DIM : (g + 1) * HEAD_DIM] = total.astype(jnp.bfloat16)
    contract = (((1,), (1,)), ((), ()))
    for i in range(chunks):
        copies = arrivals(i)
        copies[0].wait()
        total = lax.dot_general(gq_ref[...], wq[i], contract, preferred_element_type=jnp.float32)
        copies[1].wait()
        total += lax.dot_general(gk_ref[...], wk[i], contract, preferred_element_type=jnp.float32)
        copies[2].wait()
        total += lax.dot_general(gv_ref[...], wv[i], contract, preferred_element_type=jnp.float32)
        out_refs[i][...] = total.astype(jnp.bfloat16)


def projection(order, shares, gq, parts, weights):
    rows = gq.shape[0]
    chunks = order.shape[0]
    width = weights[0].shape[0] // shares
    columns = weights[1].shape[1]
    out_shape = [jax.ShapeDtypeStruct((rows, width), jnp.bfloat16)] * chunks
    if len(parts) > 2:
        out_shape = [jax.ShapeDtypeStruct((rows, columns), jnp.bfloat16)] * 2 + out_shape
    front = lambda shape: pl.BlockSpec(shape, lambda j, *_: (0, 0))
    return pl.pallas_call(
        functools.partial(projection_kernel, chunks, width, len(parts)),
        out_shape=out_shape,
        grid_spec=pltpu.PrefetchScalarGridSpec(
            num_scalar_prefetch=1,
            grid=(1,),
            in_specs=[front(gq.shape)]
            + [front((rows, part.shape[1])) for part in parts]
            + [pl.BlockSpec(memory_space=pltpu.HBM)] * 3,
            out_specs=[front(shape.shape) for shape in out_shape],
            scratch_shapes=[pltpu.VMEM((chunks, width, w.shape[1]), jnp.bfloat16) for w in weights]
            + [pltpu.SemaphoreType.DMA((chunks, 3))],
        ),
        compiler_params=pltpu.CompilerParams(vmem_limit_bytes=56 * 2**20),
        cost_estimate=pl.CostEstimate(
            flops=2 * chunks * width * rows * (gq.shape[1] + 2 * columns),
            bytes_accessed=2 * chunks * width * (gq.shape[1] + 2 * columns),
            transcendentals=0,
        ),
        name="projection",
    )(order, gq, *parts, *weights)


def bits_of(mask):
    return [1 << i for i in range(mask.bit_length()) if mask >> i & 1]


def cuts_of(rows, count):
    edges = [rows * i // count // 16 * 16 for i in range(count)] + [rows]
    return [slice(edges[i], edges[i + 1]) for i in range(count)]


def exchange(x, axis, mask):
    n = lax.axis_size(axis)
    return lax.ppermute(x, axis, [(i, i ^ mask) for i in range(n)])


def gather_pieces(own, axis):
    n = lax.axis_size(axis)
    pieces = {0: own}
    far = sorted(range(2, n, 2), key=lambda m: (m.bit_count(), m))
    for mask in far:
        bits = bits_of(mask)
        cuts = cuts_of(own.shape[0], len(bits))
        parts = [exchange(pieces[mask ^ bit][cut], axis, bit) for bit, cut in zip(bits, cuts)]
        pieces[mask] = parts[0] if len(parts) == 1 else jnp.concatenate(parts, axis=0)
    for mask in range(0, n, 2):
        pieces[mask | 1] = exchange(pieces[mask], axis, 1)
    return [pieces[k] for k in range(n)]


def scatter_parts(keep, send, axis):
    n = lax.axis_size(axis)
    rows = keep.shape[0] // (n // 2)
    got = exchange(send, axis, 1)
    parts = [keep, got]
    for mask in range(n - 2, 0, -2):
        cut = slice(mask // 2 * rows, (mask // 2 + 1) * rows)
        both = keep[cut].astype(jnp.float32) + got[cut].astype(jnp.float32)
        parts.append(exchange(both.astype(jnp.bfloat16), axis, mask))
    return parts


def line_order(n, me):
    if n == 4:
        return me ^ jnp.array([2, 3, 1, 0], jnp.int32)
    return (me + 1 + jnp.arange(n, dtype=jnp.int32)) % n


def line_sum(chunks, axis):
    n = lax.axis_size(axis)
    me = lax.axis_index(axis)
    wide = lambda x: x.astype(jnp.float32)
    if n == 4:
        first, second, third, own = chunks
        got_first = lax.ppermute(first, axis, [(0, 1), (3, 2), (1, 3), (2, 0)])
        got_second = lax.ppermute(second, axis, [(0, 3), (3, 0)])
        got_third = lax.ppermute(third, axis, [(0, 1), (2, 3), (1, 0), (3, 2)])
        passed = (wide(second) + wide(got_first)).astype(jnp.bfloat16)
        got_passed = lax.ppermute(passed, axis, [(1, 2), (2, 1)])
        outer = jnp.logical_or(me == 0, me == 3)
        total = wide(own) + jnp.where(outer, wide(got_first), 0.0)
        return (total + wide(got_second) + wide(got_third) + wide(got_passed)).astype(jnp.bfloat16)
    stacked = jnp.stack(chunks)

    def chunk(d):
        return wide(lax.dynamic_index_in_dim(stacked, (d - me - 1) % n, 0, keepdims=False))

    from_left = from_right = 0.0
    for t in range(1, n):
        right = (chunk(n - t + me) + from_left).astype(jnp.bfloat16)
        left = (chunk(t - n + me) + from_right).astype(jnp.bfloat16)
        from_left = wide(lax.ppermute(right, axis, [(i, i + 1) for i in range(t)]))
        from_right = wide(lax.ppermute(left, axis, [(n - 1 - i, n - 2 - i) for i in range(t)]))
    return (chunk(me) + from_left + from_right).astype(jnp.bfloat16)


def body(queries, keys, values, grad_out, chosen, w_query, w_key, w_value):
    groups = keys.shape[1] // HEAD_DIM
    me = lax.axis_index("ctx")
    shares = lax.axis_size("head")
    weights = (w_query, w_key, w_value)
    halves = []
    for g in range(groups):
        at = slice(g * HEAD_DIM, (g + 1) * HEAD_DIM)
        halves += [keys[:, at], values[:, at]]
    pieces = gather_pieces(jnp.concatenate(halves, axis=1), "ctx")
    grad_queries, keep, send = attention(pieces, queries, grad_out, chosen, me, 0, groups)
    parts = scatter_parts(keep, send, "ctx")
    order = line_order(shares, lax.axis_index("head"))
    grad_keys, grad_values, *chunks = projection(order[:1], shares, grad_queries, parts, weights)
    final = [grad_keys, grad_values]
    chunks += projection(order[1:2], shares, grad_queries, final, weights)
    chunks += projection(order[2:], shares, grad_queries, final, weights)
    return (grad_queries, grad_keys, grad_values, line_sum(chunks, "head"))


def solution(mesh):
    return jax.shard_map(
        body,
        mesh=mesh,
        in_specs=(
            P("ctx", "head"),
            P("ctx", "head"),
            P("ctx", "head"),
            P("ctx", "head"),
            P("ctx", "head", None),
            P(None, "head"),
            P(None, "head"),
            P(None, "head"),
        ),
        out_specs=(P("ctx", "head"), P("ctx", "head"), P("ctx", "head"), P("ctx", "head")),
        check_vma=False,
    )
```

```python
import functools
import math

import jax
import jax.numpy as jnp
from jax import lax
from jax.experimental import pallas as pl
from jax.experimental.pallas import tpu as pltpu
from jax.sharding import PartitionSpec as P

HEAD_DIM = 128
BLOCK = 64
LOG2E = math.log2(math.e)


def in_hbm(x):
    return pltpu.with_memory_space_constraint(x, pltpu.HBM)


def attention_kernel(axis, n_ctx, topk, cuts, chosen, *refs):
    pieces, (q_hbm, g_hbm, dq_hbm, *out_hbm), scratch = refs[: 2 * n_ctx], refs[2 * n_ctx : -13], refs[-13:]
    k_all, v_all, q_all, g_all, acc, near, scores, packed, operand, dq_all, staged, arrived, left = scratch
    calls = acc.shape[0]
    rows = q_hbm.shape[0]
    wide = 2 * HEAD_DIM
    width = q_hbm.shape[1] // calls
    heads_per = width // HEAD_DIM
    lanes = heads_per * BLOCK
    blocks = rows // BLOCK
    me = lax.axis_index(axis)
    scaling = 1.0 / math.sqrt(HEAD_DIM)
    step = scaling * LOG2E

    def device_rows(k, first=0, count=rows):
        return pl.ds(pl.multiple_of((me ^ k) * rows + first, 16), count)

    def arrivals(late):
        at = slice(HEAD_DIM, None) if late else slice(0, HEAD_DIM)
        copies = [] if late else [(q_hbm, q_all), (g_hbm, g_all)]
        for side, held in ((0, k_all), (1, v_all)):
            for k in range(n_ctx):
                copies.append((pieces[side * n_ctx + k].at[:, at], held.at[device_rows(k), at]))
        return [pltpu.make_async_copy(src, dst, arrived.at[late, i]) for i, (src, dst) in enumerate(copies)]

    def departures(j):
        columns = pl.ds(pl.multiple_of(j * width, HEAD_DIM), width)
        copies = [(dq_all.at[:, columns], dq_hbm.at[:, columns])]
        columns = pl.ds(pl.multiple_of(j * wide, HEAD_DIM), wide)
        first = 0
        for out in out_hbm:
            copies.append((staged.at[j, pl.ds(first, out.shape[0]), :], out.at[:, columns]))
            first += out.shape[0]
        return [pltpu.make_async_copy(src, dst, left.at[j, i]) for i, (src, dst) in enumerate(copies)]

    waves = [0] if calls == 1 else [0, 1]
    for late in waves:
        for copy in arrivals(late):
            copy.start()
    acc[...] = jnp.zeros_like(acc)
    for ref in operand:
        ref[...] = jnp.zeros_like(ref)
    offset = lax.broadcasted_iota(jnp.int32, (BLOCK, lanes), 0) - (
        lax.broadcasted_iota(jnp.int32, (BLOCK, lanes), 1) % BLOCK
    )

    def picks_of(j, b):
        own = me * blocks + b
        listed = [chosen[b, j, i] for i in range(topk)]
        return own, [own] + [jnp.where(listed[i] == own, listed[0], listed[i]) for i in range(1, topk)]

    def tile(i):
        return slice(i * BLOCK, (i + 1) * BLOCK)

    def block_rows(i):
        return pl.ds(pl.multiple_of(i * BLOCK, BLOCK), BLOCK)

    def columns_of(i):
        return pl.ds(pl.multiple_of(i * HEAD_DIM, HEAD_DIM), HEAD_DIM)

    def score_stage(j, b):
        _, picks = picks_of(j, b)
        for i in range(topk):
            near[b][tile(i), :HEAD_DIM] = k_all[block_rows(picks[i]), columns_of(j)]
            near[b][tile(i), HEAD_DIM:] = v_all[block_rows(picks[i]), columns_of(j)]
        for h in range(heads_per):
            at = columns_of(j * heads_per + h)
            operand[b][tile(h), :HEAD_DIM] = q_all[tile(b), at]
            operand[b][lanes + h * BLOCK : lanes + (h + 1) * BLOCK, HEAD_DIM:] = g_all[tile(b), at]
        scores[b][...] = lax.dot_general(
            near[b][...], operand[b][...], (((1,), (1,)), ((), ())), preferred_element_type=jnp.float32
        )

    def weight_stage(j, b):
        own, picks = picks_of(j, b)
        bias = [jnp.where(picks[i] > own, -1e30, 0.0) for i in range(topk)]
        score, weigh, pack = scores[b], scores[b], packed[b]
        first = jnp.where(offset <= 0, score[tile(0), :lanes], -1e30)
        top = first
        for i in range(1, topk):
            top = jnp.maximum(top, score[tile(i), :lanes] + bias[i])
        top = jnp.max(top, axis=0, keepdims=True)
        total = jnp.zeros((BLOCK, lanes), jnp.float32)
        delta = jnp.zeros((BLOCK, lanes), jnp.float32)
        for i in range(topk):
            s = first - top if i == 0 else score[tile(i), :lanes] - (top - bias[i])
            e = jnp.exp2(s * step)
            weigh[tile(i), :lanes] = e
            total = total + e
            delta = delta + e * score[tile(i), lanes:]
        total = 1.0 / jnp.sum(total, axis=0, keepdims=True)
        delta = jnp.sum(delta, axis=0, keepdims=True) * total
        for i in range(topk):
            w = weigh[tile(i), :lanes] * total
            pack[tile(i), lanes:] = w.astype(jnp.bfloat16)
            pack[tile(i), :lanes] = (w * (score[tile(i), lanes:] - delta)).astype(jnp.bfloat16)

    def term_stage(j, b):
        _, picks = picks_of(j, b)
        terms = jnp.dot(packed[b][...], operand[b][...], preferred_element_type=jnp.float32)
        for i in range(topk):
            acc[j, block_rows(picks[i]), :] += terms[tile(i), :]
        dq = scaling * lax.dot_general(
            packed[b][:, :lanes],
            near[b][:, :HEAD_DIM],
            (((0,), (0,)), ((), ())),
            preferred_element_type=jnp.float32,
        )
        dq = dq.astype(jnp.bfloat16)
        for h in range(heads_per):
            dq_all[tile(b), columns_of(j * heads_per + h)] = dq[tile(h), :]

    def leave(j):
        first = 0
        for cut in cuts:
            count = cut.stop - cut.start
            for core in range(2):
                for k in range(n_ctx // 2):
                    at = device_rows(2 * k + core, cut.start, count)
                    to = slice(first, first + count)
                    staged[j, to, :HEAD_DIM] = (acc[j, at, :HEAD_DIM] * scaling).astype(jnp.bfloat16)
                    staged[j, to, HEAD_DIM:] = acc[j, at, HEAD_DIM:].astype(jnp.bfloat16)
                    first += count
        for copy in departures(j):
            copy.start()

    def run(group, b, scoring=True, weighing=True, summing=True):
        if scoring:
            score_stage(group + b // blocks, b % blocks)
        if weighing:
            weight_stage(group + (b - 1) // blocks, (b - 1) % blocks)
        if summing:
            term_stage(group + (b - 2) // blocks, (b - 2) % blocks)

    def one_group(group, carry):
        for b in range(2, blocks + 2):
            run(group, b)
        leave(group)
        return carry

    for copy in arrivals(0):
        copy.wait()
    run(0, 0, weighing=False, summing=False)
    run(0, 1, summing=False)
    for late in waves[1:]:
        for copy in arrivals(late):
            copy.wait()
    lax.fori_loop(0, calls - 1, one_group, 0)
    for b in range(2, blocks):
        run(calls - 1, b)
    run(calls - 1, blocks, scoring=False)
    run(calls - 1, blocks + 1, scoring=False, weighing=False)
    leave(calls - 1)
    for j in range(calls):
        for copy in departures(j):
            copy.wait()


def attention(axis, pieces, queries, grad_out, chosen, cuts):
    n_ctx = len(pieces) // 2
    rows = queries.shape[0]
    topk = chosen.shape[-1]
    wide = 2 * HEAD_DIM
    groups = pieces[0].shape[1] // HEAD_DIM
    width = queries.shape[1] // groups
    lanes = width // HEAD_DIM * BLOCK
    blocks = rows // BLOCK
    near = topk * BLOCK
    flops = groups * blocks * 10 * near * lanes * HEAD_DIM
    sizes = [n_ctx // 2 * (cut.stop - cut.start) for cut in cuts for core in range(2)]
    bf16 = lambda *shape: pltpu.VMEM(shape, jnp.bfloat16)
    f32 = lambda *shape: pltpu.VMEM(shape, jnp.float32)
    anywhere = pl.BlockSpec(memory_space=pl.ANY)
    return pl.pallas_call(
        functools.partial(attention_kernel, axis, n_ctx, topk, cuts),
        out_shape=[jax.ShapeDtypeStruct(queries.shape, jnp.bfloat16)]
        + [jax.ShapeDtypeStruct((size, groups * wide), jnp.bfloat16) for size in sizes],
        grid_spec=pltpu.PrefetchScalarGridSpec(
            num_scalar_prefetch=1,
            grid=(1,),
            in_specs=[anywhere] * (2 * n_ctx + 2),
            out_specs=[anywhere] * (1 + len(sizes)),
            scratch_shapes=[
                bf16(n_ctx * rows, groups * HEAD_DIM),
                bf16(n_ctx * rows, groups * HEAD_DIM),
                bf16(*queries.shape),
                bf16(*queries.shape),
                f32(groups, n_ctx * rows, wide),
                [bf16(near, wide)] * blocks,
                [f32(near, 2 * lanes)] * blocks,
                [bf16(near, 2 * lanes)] * blocks,
                [bf16(2 * lanes, wide)] * blocks,
                bf16(*queries.shape),
                bf16(groups, n_ctx * rows, wide),
                pltpu.SemaphoreType.DMA((2, 2 * n_ctx + 2)),
                pltpu.SemaphoreType.DMA((groups, 1 + len(sizes))),
            ],
        ),
        compiler_params=pltpu.CompilerParams(vmem_limit_bytes=36 * 2**20),
        cost_estimate=pl.CostEstimate(flops=flops, bytes_accessed=16 * n_ctx * rows * wide * groups, transcendentals=0),
        name="attention",
    )(chosen, *pieces, in_hbm(queries), in_hbm(grad_out))


def query_term_kernel(gq_ref, w_ref, out_ref):
    out_ref[...] = lax.dot_general(
        gq_ref[...], w_ref[...], (((1,), (1,)), ((), ())), preferred_element_type=jnp.float32
    ).astype(jnp.bfloat16)


def query_term(shares, gq, w):
    rows, depth = gq.shape
    width = w.shape[0] // shares
    return pl.pallas_call(
        query_term_kernel,
        out_shape=jax.ShapeDtypeStruct((shares, rows, width), jnp.bfloat16),
        grid=(shares,),
        in_specs=[pl.BlockSpec((rows, depth), lambda j: (0, 0)), pl.BlockSpec((width, depth), lambda j: (j, 0))],
        out_specs=pl.BlockSpec((None, rows, width), lambda j: (j, 0, 0)),
        compiler_params=pltpu.CompilerParams(vmem_limit_bytes=16 * 2**20),
        cost_estimate=pl.CostEstimate(
            flops=2 * shares * width * rows * depth, bytes_accessed=2 * shares * width * depth, transcendentals=0
        ),
        name="query_term",
    )(gq, w)


def projection_kernel(axis, places, cut, summed, *refs):
    count = len(places)
    parts, (term, wk_hbm, wv_hbm), refs = refs[:summed], refs[summed : summed + 3], refs[summed + 3 :]
    if summed > 2:
        gk_hbm, gv_hbm, *refs = refs
    out_hbm, (wk, wv, terms, held, gk, gv, out, w_sem, part_sem, out_sem) = refs[:count], refs[count:]
    width = wk.shape[1]
    rows = cut.stop - cut.start
    n = lax.axis_size(axis)
    order = [line_order(n, lax.axis_index(axis))[i] for i in places]

    def arrivals(i):
        at = pl.ds(pl.multiple_of(order[i] * width, width), width)
        copies = ((wk_hbm.at[at, :], wk), (wv_hbm.at[at, :], wv), (term.at[order[i], pl.ds(cut.start, rows), :], terms))
        return [pltpu.make_async_copy(src, dst.at[i], w_sem.at[i, k]) for k, (src, dst) in enumerate(copies)]

    targets = [held.at[i] for i in range(summed)] if summed > 2 else [gk, gv]
    part_copies = [
        pltpu.make_async_copy(src.at[pl.ds(0, rows), :], dst, part_sem.at[i])
        for i, (src, dst) in enumerate(zip(parts, targets))
    ]
    for copy in part_copies:
        copy.start()
    for i in range(count):
        for copy in arrivals(i):
            copy.start()
    for copy in part_copies:
        copy.wait()
    leaving = []

    def leave(src, dst):
        leaving.append(pltpu.make_async_copy(src, dst, out_sem.at[len(leaving)]))
        leaving[-1].start()

    if summed > 2:
        for g in range(gk.shape[1] // HEAD_DIM):
            for side, total_ref in ((0, gk), (1, gv)):
                at = slice((2 * g + side) * HEAD_DIM, (2 * g + side + 1) * HEAD_DIM)
                total = held[0, :, at].astype(jnp.float32)
                for i in range(1, summed):
                    total += held[i, :, at].astype(jnp.float32)
                total_ref[:, g * HEAD_DIM : (g + 1) * HEAD_DIM] = total.astype(jnp.bfloat16)
        leave(gk, gk_hbm)
        leave(gv, gv_hbm)
    contract = (((1,), (1,)), ((), ()))
    for i in range(count):
        for copy in arrivals(i):
            copy.wait()
        total = terms[i].astype(jnp.float32)
        total += lax.dot_general(gk[...], wk[i], contract, preferred_element_type=jnp.float32)
        total += lax.dot_general(gv[...], wv[i], contract, preferred_element_type=jnp.float32)
        out[i] = total.astype(jnp.bfloat16)
        leave(out.at[i], out_hbm[i])
    for copy in leaving:
        copy.wait()


def projection(axis, places, cut, parts, term, weights):
    count = len(places)
    summed = len(parts)
    rows = cut.stop - cut.start
    columns = weights[0].shape[1]
    width = term.shape[2]
    out_shape = [jax.ShapeDtypeStruct((rows, width), jnp.bfloat16)] * count
    if summed > 2:
        out_shape = [jax.ShapeDtypeStruct((rows, columns), jnp.bfloat16)] * 2 + out_shape
    bf16 = lambda *shape: pltpu.VMEM(shape, jnp.bfloat16)
    anywhere = pl.BlockSpec(memory_space=pl.ANY)
    return pl.pallas_call(
        functools.partial(projection_kernel, axis, places, cut, summed),
        out_shape=out_shape,
        in_specs=[anywhere] * (summed + 3),
        out_specs=[anywhere] * len(out_shape),
        scratch_shapes=[
            bf16(count, width, columns),
            bf16(count, width, columns),
            bf16(count, rows, width),
            bf16(summed, rows, parts[0].shape[1]),
            bf16(rows, columns),
            bf16(rows, columns),
            bf16(count, rows, width),
            pltpu.SemaphoreType.DMA((count, 3)),
            pltpu.SemaphoreType.DMA((summed,)),
            pltpu.SemaphoreType.DMA((len(out_shape),)),
        ],
        compiler_params=pltpu.CompilerParams(vmem_limit_bytes=16 * 2**20),
        cost_estimate=pl.CostEstimate(
            flops=4 * count * width * rows * columns, bytes_accessed=4 * count * width * columns, transcendentals=0
        ),
        name="projection",
    )(*parts, term, *map(in_hbm, weights))


def exchange(x, axis, mask):
    n = lax.axis_size(axis)
    return lax.ppermute(x, axis, [(i, i ^ mask) for i in range(n)])


def gather_pieces(sides, axis):
    n = lax.axis_size(axis)
    pieces = [{0: side} for side in sides]
    for mask in sorted(range(2, n, 2), key=lambda m: (m.bit_count(), m)):
        bits = [1 << i for i in range(n.bit_length()) if mask >> i & 1]
        for i, held in enumerate(pieces):
            bit = bits[(i - 1) % len(bits)]
            held[mask] = exchange(held[mask ^ bit], axis, bit)
    for held in pieces:
        for mask in range(0, n, 2):
            held[mask | 1] = exchange(held[mask], axis, 1)
    return [held[k] for held in pieces for k in range(n)]


def scatter_parts(keep, got, axis):
    n = lax.axis_size(axis)
    rows = keep.shape[0] // (n // 2)
    sums = {}
    for mask in range(n - 2, 0, -2):
        cut = slice(mask // 2 * rows, (mask // 2 + 1) * rows)
        sums[mask] = (keep[cut].astype(jnp.float32) + got[cut].astype(jnp.float32)).astype(jnp.bfloat16)
    return [keep, got] + [exchange(x, axis, mask) for mask, x in sums.items()], list(sums.values())


def line_order(n, me):
    if n == 4:
        return [me ^ 2, me ^ 3, me ^ 1, me]
    return [(me + 1 + i) % n for i in range(n)]


def line_sum(chunks, axis, after):
    n = lax.axis_size(axis)
    me = lax.axis_index(axis)
    wide = lambda x: x.astype(jnp.float32)
    if after:
        chunks[1:], _ = lax.optimization_barrier((chunks[1:], after))
    if n == 4:
        first, second, third, own = chunks
        got_first = lax.ppermute(first, axis, [(0, 1), (3, 2), (1, 3), (2, 0)])
        got_second = lax.ppermute(second, axis, [(0, 3), (3, 0)])
        got_third = lax.ppermute(third, axis, [(0, 1), (2, 3), (1, 0), (3, 2)])
        passed = (wide(second) + wide(got_first)).astype(jnp.bfloat16)
        got_passed = lax.ppermute(passed, axis, [(1, 2), (2, 1)])
        outer = jnp.logical_or(me == 0, me == 3)
        total = wide(own) + jnp.where(outer, wide(got_first), 0.0)
        return (total + wide(got_second) + wide(got_third) + wide(got_passed)).astype(jnp.bfloat16), [
            got_first,
            got_second,
            got_third,
        ]
    stacked = jnp.stack(chunks)

    def chunk(d):
        return wide(lax.dynamic_index_in_dim(stacked, (d - me - 1) % n, 0, keepdims=False))

    from_left = from_right = 0.0
    for t in range(1, n):
        right = (chunk(n - t + me) + from_left).astype(jnp.bfloat16)
        left = (chunk(t - n + me) + from_right).astype(jnp.bfloat16)
        from_left = wide(lax.ppermute(right, axis, [(i, i + 1) for i in range(t)]))
        from_right = wide(lax.ppermute(left, axis, [(n - 1 - i, n - 2 - i) for i in range(t)]))
    return (chunk(me) + from_left + from_right).astype(jnp.bfloat16), [from_left, from_right]


def body(queries, keys, values, grad_out, chosen, w_query, w_key, w_value):
    rows = queries.shape[0]
    front = rows * 3 // 8 // 16 * 16
    cuts = [slice(0, front), slice(front, rows)]
    shares = lax.axis_size("head")
    pieces = gather_pieces((keys, values), "ctx")
    pieces[0], pieces[len(pieces) // 2] = in_hbm(keys), in_hbm(values)
    grad_queries, *terms = attention("ctx", pieces, queries, grad_out, chosen, cuts)
    held = [(keep, exchange(send, "ctx", 1)) for keep, send in zip(terms[::2], terms[1::2])]
    term = query_term(shares, grad_queries, w_query)
    weights = (w_key, w_value)
    received = []
    sent = []
    for keep, got in held:
        if sent:
            keep, got, _ = lax.optimization_barrier((keep, got, sent))
        arrived, sent = scatter_parts(keep, got, "ctx")
        received.append(arrived)
    grads = []
    after = []
    for cut, arrived in zip(cuts, received):
        grad_k, grad_v, *chunks = projection("head", range(shares // 2), cut, arrived, term, weights)
        chunks += projection("head", range(shares // 2, shares), cut, [grad_k, grad_v], term, weights)
        total, after = line_sum(chunks, "head", after)
        grads.append((grad_k, grad_v, total))
    grad_keys, grad_values, grad_input = (jnp.concatenate(halves, axis=0) for halves in zip(*grads))
    return (grad_queries, grad_keys, grad_values, grad_input)


def solution(mesh):
    return jax.shard_map(
        body,
        mesh=mesh,
        in_specs=(
            P("ctx", "head"),
            P("ctx", "head"),
            P("ctx", "head"),
            P("ctx", "head"),
            P("ctx", "head", None),
            P(None, "head"),
            P(None, "head"),
            P(None, "head"),
        ),
        out_specs=(P("ctx", "head"), P("ctx", "head"), P("ctx", "head"), P("ctx", "head")),
        check_vma=False,
    )
```

```python
import functools
import math

import jax
import jax.numpy as jnp
from jax import lax
from jax.experimental import pallas as pl
from jax.experimental.pallas import tpu as pltpu
from jax.sharding import PartitionSpec as P

HEAD_DIM = 128
BLOCK = 64
LOG2E = math.log2(math.e)


def in_hbm(x):
    return pltpu.with_memory_space_constraint(x, pltpu.HBM)


def attention_kernel(axis, n_ctx, topk, cuts, chosen_hbm, *refs):
    pieces, (q_hbm, g_hbm, dq_hbm, *out_hbm), scratch = refs[: 2 * n_ctx], refs[2 * n_ctx : -14], refs[-14:]
    k_all, v_all, q_all, g_all, acc, near, scores, packed, operand, dq_all, staged, chosen, arrived, left = scratch
    calls = acc.shape[0]
    rows = q_hbm.shape[0]
    wide = 2 * HEAD_DIM
    width = q_hbm.shape[1] // calls
    heads_per = width // HEAD_DIM
    lanes = heads_per * BLOCK
    blocks = rows // BLOCK
    me = lax.axis_index(axis)
    scaling = 1.0 / math.sqrt(HEAD_DIM)
    step = scaling * LOG2E

    def device_rows(k, first=0, count=rows):
        return pl.ds(pl.multiple_of((me ^ k) * rows + first, 16), count)

    def arrivals(late):
        at = slice(HEAD_DIM, None) if late else slice(0, HEAD_DIM)
        copies = [] if late else [(chosen_hbm, chosen), (q_hbm, q_all), (g_hbm, g_all)]
        for side, held in ((0, k_all), (1, v_all)):
            for k in range(n_ctx):
                copies.append((pieces[side * n_ctx + k].at[:, at], held.at[device_rows(k), at]))
        return [pltpu.make_async_copy(src, dst, arrived.at[late, i]) for i, (src, dst) in enumerate(copies)]

    def departures(j):
        columns = pl.ds(pl.multiple_of(j * width, HEAD_DIM), width)
        copies = [(dq_all.at[:, columns], dq_hbm.at[:, columns])]
        columns = pl.ds(pl.multiple_of(j * wide, HEAD_DIM), wide)
        first = 0
        for out in out_hbm:
            copies.append((staged.at[j, pl.ds(first, out.shape[0]), :], out.at[:, columns]))
            first += out.shape[0]
        return [pltpu.make_async_copy(src, dst, left.at[j, i]) for i, (src, dst) in enumerate(copies)]

    waves = [0] if calls == 1 else [0, 1]
    for late in waves:
        for copy in arrivals(late):
            copy.start()
    acc[...] = jnp.zeros_like(acc)
    for ref in operand:
        ref[...] = jnp.zeros_like(ref)
    offset = lax.broadcasted_iota(jnp.int32, (BLOCK, lanes), 0) - (
        lax.broadcasted_iota(jnp.int32, (BLOCK, lanes), 1) % BLOCK
    )

    def picks_of(j, b):
        own = me * blocks + b
        listed = [chosen[b, j, i] for i in range(topk)]
        return own, [own] + [jnp.where(listed[i] == own, listed[0], listed[i]) for i in range(1, topk)]

    def tile(i):
        return slice(i * BLOCK, (i + 1) * BLOCK)

    def block_rows(i):
        return pl.ds(pl.multiple_of(i * BLOCK, BLOCK), BLOCK)

    def columns_of(i):
        return pl.ds(pl.multiple_of(i * HEAD_DIM, HEAD_DIM), HEAD_DIM)

    def score_stage(j, b):
        _, picks = picks_of(j, b)
        for i in range(topk):
            near[b][tile(i), :HEAD_DIM] = k_all[block_rows(picks[i]), columns_of(j)]
            near[b][tile(i), HEAD_DIM:] = v_all[block_rows(picks[i]), columns_of(j)]
        for h in range(heads_per):
            at = columns_of(j * heads_per + h)
            operand[b][tile(h), :HEAD_DIM] = q_all[tile(b), at]
            operand[b][lanes + h * BLOCK : lanes + (h + 1) * BLOCK, HEAD_DIM:] = g_all[tile(b), at]
        scores[b][...] = lax.dot_general(
            near[b][...], operand[b][...], (((1,), (1,)), ((), ())), preferred_element_type=jnp.float32
        )

    def weight_stage(j, b):
        own, picks = picks_of(j, b)
        bias = [jnp.where(picks[i] > own, -1e30, 0.0) for i in range(topk)]
        score, weigh, pack = scores[b], scores[b], packed[b]
        first = jnp.where(offset <= 0, score[tile(0), :lanes], -1e30)
        top = first
        for i in range(1, topk):
            top = jnp.maximum(top, score[tile(i), :lanes] + bias[i])
        top = jnp.max(top, axis=0, keepdims=True)
        total = jnp.zeros((BLOCK, lanes), jnp.float32)
        delta = jnp.zeros((BLOCK, lanes), jnp.float32)
        for i in range(topk):
            s = first - top if i == 0 else score[tile(i), :lanes] - (top - bias[i])
            e = jnp.exp2(s * step)
            weigh[tile(i), :lanes] = e
            total = total + e
            delta = delta + e * score[tile(i), lanes:]
        total = 1.0 / jnp.sum(total, axis=0, keepdims=True)
        delta = jnp.sum(delta, axis=0, keepdims=True) * total
        for i in range(topk):
            w = weigh[tile(i), :lanes] * total
            pack[tile(i), lanes:] = w.astype(jnp.bfloat16)
            pack[tile(i), :lanes] = (w * (score[tile(i), lanes:] - delta)).astype(jnp.bfloat16)

    def term_stage(j, b):
        _, picks = picks_of(j, b)
        terms = jnp.dot(packed[b][...], operand[b][...], preferred_element_type=jnp.float32)
        for i in range(topk):
            acc[j, block_rows(picks[i]), :] += terms[tile(i), :]
        dq = scaling * lax.dot_general(
            near[b][:, :HEAD_DIM],
            packed[b][:, :lanes],
            (((0,), (0,)), ((), ())),
            preferred_element_type=jnp.float32,
        )
        dq = dq.T.astype(jnp.bfloat16)
        for h in range(heads_per):
            dq_all[tile(b), columns_of(j * heads_per + h)] = dq[tile(h), :]

    def leave(j):
        first = 0
        for cut in cuts:
            count = cut.stop - cut.start
            for core in range(2):
                for k in range(n_ctx // 2):
                    at = device_rows(2 * k + core, cut.start, count)
                    to = slice(first, first + count)
                    staged[j, to, :HEAD_DIM] = (acc[j, at, :HEAD_DIM] * scaling).astype(jnp.bfloat16)
                    staged[j, to, HEAD_DIM:] = acc[j, at, HEAD_DIM:].astype(jnp.bfloat16)
                    first += count
        for copy in departures(j):
            copy.start()

    def run(group, b, scoring=True, weighing=True, summing=True):
        if scoring:
            score_stage(group + b // blocks, b % blocks)
        if weighing:
            weight_stage(group + (b - 1) // blocks, (b - 1) % blocks)
        if summing:
            term_stage(group + (b - 2) // blocks, (b - 2) % blocks)

    def one_group(group, carry):
        for b in range(2, blocks + 2):
            run(group, b)
        leave(group)
        return carry

    for copy in arrivals(0):
        copy.wait()
    run(0, 0, weighing=False, summing=False)
    run(0, 1, summing=False)
    for late in waves[1:]:
        for copy in arrivals(late):
            copy.wait()
    lax.fori_loop(0, calls - 1, one_group, 0)
    for b in range(2, blocks):
        run(calls - 1, b)
    run(calls - 1, blocks, scoring=False)
    run(calls - 1, blocks + 1, scoring=False, weighing=False)
    leave(calls - 1)
    for j in range(calls):
        for copy in departures(j):
            copy.wait()


def attention(axis, pieces, queries, grad_out, chosen, cuts):
    n_ctx = len(pieces) // 2
    rows = queries.shape[0]
    topk = chosen.shape[-1]
    wide = 2 * HEAD_DIM
    groups = pieces[0].shape[1] // HEAD_DIM
    width = queries.shape[1] // groups
    lanes = width // HEAD_DIM * BLOCK
    blocks = rows // BLOCK
    near = topk * BLOCK
    flops = groups * blocks * 10 * near * lanes * HEAD_DIM
    sizes = [n_ctx // 2 * (cut.stop - cut.start) for cut in cuts for core in range(2)]
    bf16 = lambda *shape: pltpu.VMEM(shape, jnp.bfloat16)
    f32 = lambda *shape: pltpu.VMEM(shape, jnp.float32)
    anywhere = pl.BlockSpec(memory_space=pl.ANY)
    return pl.pallas_call(
        functools.partial(attention_kernel, axis, n_ctx, topk, cuts),
        out_shape=[jax.ShapeDtypeStruct(queries.shape, jnp.bfloat16)]
        + [jax.ShapeDtypeStruct((size, groups * wide), jnp.bfloat16) for size in sizes],
        in_specs=[anywhere] * (2 * n_ctx + 3),
        out_specs=[anywhere] * (1 + len(sizes)),
        scratch_shapes=[
            bf16(n_ctx * rows, groups * HEAD_DIM),
            bf16(n_ctx * rows, groups * HEAD_DIM),
            bf16(*queries.shape),
            bf16(*queries.shape),
            f32(groups, n_ctx * rows, wide),
            [bf16(near, wide)] * blocks,
            [f32(near, 2 * lanes)] * blocks,
            [bf16(near, 2 * lanes)] * blocks,
            [bf16(2 * lanes, wide)] * blocks,
            bf16(*queries.shape),
            bf16(groups, n_ctx * rows, wide),
            pltpu.SMEM(chosen.shape, jnp.int32),
            pltpu.SemaphoreType.DMA((2, 2 * n_ctx + 3)),
            pltpu.SemaphoreType.DMA((groups, 1 + len(sizes))),
        ],
        compiler_params=pltpu.CompilerParams(vmem_limit_bytes=28 * 2**20),
        cost_estimate=pl.CostEstimate(flops=flops, bytes_accessed=16 * n_ctx * rows * wide * groups, transcendentals=0),
        name="attention",
    )(in_hbm(chosen), *pieces, in_hbm(queries), in_hbm(grad_out))


def query_term_kernel(gq_ref, w_ref, out_ref):
    out_ref[...] = lax.dot_general(
        gq_ref[...], w_ref[...], (((1,), (1,)), ((), ())), preferred_element_type=jnp.float32
    ).astype(jnp.bfloat16)


def query_term(shares, gq, w):
    rows, depth = gq.shape
    width = w.shape[0] // shares
    return pl.pallas_call(
        query_term_kernel,
        out_shape=jax.ShapeDtypeStruct((shares, rows, width), jnp.bfloat16),
        grid=(shares,),
        in_specs=[pl.BlockSpec((rows, depth), lambda j: (0, 0)), pl.BlockSpec((width, depth), lambda j: (j, 0))],
        out_specs=pl.BlockSpec((None, rows, width), lambda j: (j, 0, 0)),
        compiler_params=pltpu.CompilerParams(vmem_limit_bytes=16 * 2**20),
        cost_estimate=pl.CostEstimate(
            flops=2 * shares * width * rows * depth, bytes_accessed=2 * shares * width * depth, transcendentals=0
        ),
        name="query_term",
    )(gq, w)


def projection_kernel(axis, places, cut, summed, *refs):
    count = len(places)
    parts, (term, wk_hbm, wv_hbm), refs = refs[:summed], refs[summed : summed + 3], refs[summed + 3 :]
    if summed > 2:
        gk_hbm, gv_hbm, *refs = refs
    out_hbm, (wk, wv, terms, held, gk, gv, out, w_sem, part_sem, out_sem) = refs[:count], refs[count:]
    width = wk.shape[1]
    rows = cut.stop - cut.start
    n = lax.axis_size(axis)
    order = [line_order(n, lax.axis_index(axis))[i] for i in places]

    def arrivals(i):
        at = pl.ds(pl.multiple_of(order[i] * width, width), width)
        copies = ((wk_hbm.at[at, :], wk), (wv_hbm.at[at, :], wv), (term.at[order[i], pl.ds(cut.start, rows), :], terms))
        return [pltpu.make_async_copy(src, dst.at[i], w_sem.at[i, k]) for k, (src, dst) in enumerate(copies)]

    targets = [held.at[i] for i in range(summed)] if summed > 2 else [gk, gv]
    part_copies = [
        pltpu.make_async_copy(src.at[pl.ds(0, rows), :], dst, part_sem.at[i])
        for i, (src, dst) in enumerate(zip(parts, targets))
    ]
    for copy in part_copies:
        copy.start()
    for i in range(count):
        for copy in arrivals(i):
            copy.start()
    for copy in part_copies:
        copy.wait()
    leaving = []

    def leave(src, dst):
        leaving.append(pltpu.make_async_copy(src, dst, out_sem.at[len(leaving)]))
        leaving[-1].start()

    if summed > 2:
        for g in range(gk.shape[1] // HEAD_DIM):
            for side, total_ref in ((0, gk), (1, gv)):
                at = slice((2 * g + side) * HEAD_DIM, (2 * g + side + 1) * HEAD_DIM)
                total = held[0, :, at].astype(jnp.float32)
                for i in range(1, summed):
                    total += held[i, :, at].astype(jnp.float32)
                total_ref[:, g * HEAD_DIM : (g + 1) * HEAD_DIM] = total.astype(jnp.bfloat16)
        leave(gk, gk_hbm)
        leave(gv, gv_hbm)
    contract = (((1,), (1,)), ((), ()))
    for i in range(count):
        for copy in arrivals(i):
            copy.wait()
        total = terms[i].astype(jnp.float32)
        total += lax.dot_general(gk[...], wk[i], contract, preferred_element_type=jnp.float32)
        total += lax.dot_general(gv[...], wv[i], contract, preferred_element_type=jnp.float32)
        out[i] = total.astype(jnp.bfloat16)
        leave(out.at[i], out_hbm[i])
    for copy in leaving:
        copy.wait()


def projection(axis, places, cut, parts, term, weights):
    count = len(places)
    summed = len(parts)
    rows = cut.stop - cut.start
    columns = weights[0].shape[1]
    width = term.shape[2]
    out_shape = [pltpu.HBM((rows, width), jnp.bfloat16)] * count
    if summed > 2:
        out_shape = [jax.ShapeDtypeStruct((rows, columns), jnp.bfloat16)] * 2 + out_shape
    bf16 = lambda *shape: pltpu.VMEM(shape, jnp.bfloat16)
    anywhere = pl.BlockSpec(memory_space=pl.ANY)
    return pl.pallas_call(
        functools.partial(projection_kernel, axis, places, cut, summed),
        out_shape=out_shape,
        in_specs=[anywhere] * (summed + 3),
        out_specs=[anywhere] * len(out_shape),
        scratch_shapes=[
            bf16(count, width, columns),
            bf16(count, width, columns),
            bf16(count, rows, width),
            bf16(summed, rows, parts[0].shape[1]),
            bf16(rows, columns),
            bf16(rows, columns),
            bf16(count, rows, width),
            pltpu.SemaphoreType.DMA((count, 3)),
            pltpu.SemaphoreType.DMA((summed,)),
            pltpu.SemaphoreType.DMA((len(out_shape),)),
        ],
        compiler_params=pltpu.CompilerParams(vmem_limit_bytes=16 * 2**20),
        cost_estimate=pl.CostEstimate(
            flops=4 * count * width * rows * columns, bytes_accessed=4 * count * width * columns, transcendentals=0
        ),
        name="projection",
    )(*parts, term, *map(in_hbm, weights))


def exchange(x, axis, mask):
    n = lax.axis_size(axis)
    return lax.ppermute(x, axis, [(i, i ^ mask) for i in range(n)])


def gather_pieces(sides, axis):
    n = lax.axis_size(axis)
    pieces = [{0: side} for side in sides]
    for mask in sorted(range(2, n, 2), key=lambda m: (m.bit_count(), m)):
        bits = [1 << i for i in range(n.bit_length()) if mask >> i & 1]
        for i, held in enumerate(pieces):
            bit = bits[(i - 1) % len(bits)]
            held[mask] = exchange(held[mask ^ bit], axis, bit)
    for held in pieces:
        for mask in range(0, n, 2):
            held[mask | 1] = exchange(held[mask], axis, 1)
    return [held[k] for held in pieces for k in range(n)]


def scatter_parts(keep, got, axis):
    n = lax.axis_size(axis)
    rows = keep.shape[0] // (n // 2)
    sums = {}
    for mask in range(n - 2, 0, -2):
        cut = slice(mask // 2 * rows, (mask // 2 + 1) * rows)
        sums[mask] = (keep[cut].astype(jnp.float32) + got[cut].astype(jnp.float32)).astype(jnp.bfloat16)
    return [keep, got] + [exchange(x, axis, mask) for mask, x in sums.items()], list(sums.values())


def line_order(n, me):
    if n == 4:
        return [me ^ 2, me ^ 3, me ^ 1, me]
    return [(me + 1 + i) % n for i in range(n)]


def line_sum(chunks, axis, after):
    n = lax.axis_size(axis)
    me = lax.axis_index(axis)
    wide = lambda x: x.astype(jnp.float32)
    if after:
        chunks[1:], _ = lax.optimization_barrier((chunks[1:], after))
    if n == 4:
        first, second, third, own = chunks
        got_first = lax.ppermute(first, axis, [(0, 1), (3, 2), (1, 3), (2, 0)])
        got_second = lax.ppermute(second, axis, [(0, 3), (3, 0)])
        got_third = lax.ppermute(third, axis, [(0, 1), (2, 3), (1, 0), (3, 2)])
        passed = (wide(second) + wide(got_first)).astype(jnp.bfloat16)
        got_passed = lax.ppermute(passed, axis, [(1, 2), (2, 1)])
        outer = jnp.logical_or(me == 0, me == 3)
        total = wide(own) + jnp.where(outer, wide(got_first), 0.0)
        return (total + wide(got_second) + wide(got_third) + wide(got_passed)).astype(jnp.bfloat16), [
            got_first,
            got_second,
            got_third,
        ]
    stacked = jnp.stack(chunks)

    def chunk(d):
        return wide(lax.dynamic_index_in_dim(stacked, (d - me - 1) % n, 0, keepdims=False))

    from_left = from_right = 0.0
    for t in range(1, n):
        right = (chunk(n - t + me) + from_left).astype(jnp.bfloat16)
        left = (chunk(t - n + me) + from_right).astype(jnp.bfloat16)
        from_left = wide(lax.ppermute(right, axis, [(i, i + 1) for i in range(t)]))
        from_right = wide(lax.ppermute(left, axis, [(n - 1 - i, n - 2 - i) for i in range(t)]))
    return (chunk(me) + from_left + from_right).astype(jnp.bfloat16), [from_left, from_right]


def body(queries, keys, values, grad_out, chosen, w_query, w_key, w_value):
    rows = queries.shape[0]
    front = rows * 5 // 16 // 16 * 16
    cuts = [slice(0, front), slice(front, rows)]
    shares = lax.axis_size("head")
    pieces = gather_pieces((keys, values), "ctx")
    pieces[0], pieces[len(pieces) // 2] = in_hbm(keys), in_hbm(values)
    grad_queries, *terms = attention("ctx", pieces, queries, grad_out, chosen, cuts)
    held = []
    for keep, send in zip(terms[::2], terms[1::2]):
        if held:
            send, _ = lax.optimization_barrier((send, held[-1][1]))
        held.append((keep, exchange(send, "ctx", 1)))
    term = query_term(shares, grad_queries, w_query)
    weights = (w_key, w_value)
    received = []
    sent = []
    for keep, got in held:
        if sent:
            keep, got, _ = lax.optimization_barrier((keep, got, sent))
        arrived, sent = scatter_parts(keep, got, "ctx")
        received.append(arrived)
    grads = []
    after = []
    for cut, arrived in zip(cuts, received):
        early = shares // 2
        grad_k, grad_v, *chunks = projection("head", range(early), cut, arrived, term, weights)
        chunks += projection("head", range(early, shares), cut, [grad_k, grad_v], term, weights)
        total, after = line_sum(chunks, "head", after)
        grads.append((grad_k, grad_v, total))
    grad_keys, grad_values, grad_input = (
        lax.dynamic_update_slice(jnp.pad(head, ((0, tail.shape[0]), (0, 0))), tail, (head.shape[0], 0))
        for head, tail in zip(*grads)
    )
    return (grad_queries, grad_keys, grad_values, grad_input)


def solution(mesh):
    return jax.shard_map(
        body,
        mesh=mesh,
        in_specs=(
            P("ctx", "head"),
            P("ctx", "head"),
            P("ctx", "head"),
            P("ctx", "head"),
            P("ctx", "head", None),
            P(None, "head"),
            P(None, "head"),
            P(None, "head"),
        ),
        out_specs=(P("ctx", "head"), P("ctx", "head"), P("ctx", "head"), P("ctx", "head")),
        check_vma=False,
    )
```

```python
import functools
import math

import jax
import jax.numpy as jnp
from jax import lax
from jax.experimental import pallas as pl
from jax.experimental.pallas import tpu as pltpu
from jax.sharding import PartitionSpec as P

HEAD_DIM = 128
BLOCK = 64
LOG2E = math.log2(math.e)


def in_hbm(x):
    return pltpu.with_memory_space_constraint(x, pltpu.HBM)


def attention_kernel(axis, n_ctx, topk, cuts, chosen_hbm, *refs):
    pieces, (q_hbm, g_hbm, dq_hbm, *out_hbm), scratch = refs[: 2 * n_ctx], refs[2 * n_ctx : -14], refs[-14:]
    k_all, v_all, q_all, g_all, acc, near, scores, packed, operand, dq_all, staged, chosen, arrived, left = scratch
    calls = acc.shape[0]
    rows = q_hbm.shape[0]
    wide = 2 * HEAD_DIM
    width = q_hbm.shape[1] // calls
    heads_per = width // HEAD_DIM
    lanes = heads_per * BLOCK
    blocks = rows // BLOCK
    me = lax.axis_index(axis)
    scaling = 1.0 / math.sqrt(HEAD_DIM)
    step = scaling * LOG2E

    def device_rows(k, first=0, count=rows):
        return pl.ds(pl.multiple_of((me ^ k) * rows + first, 16), count)

    def arrivals(late):
        at = slice(HEAD_DIM, None) if late else slice(0, HEAD_DIM)
        copies = [] if late else [(chosen_hbm, chosen), (q_hbm, q_all), (g_hbm, g_all)]
        for side, held in ((0, k_all), (1, v_all)):
            for k in range(n_ctx):
                copies.append((pieces[side * n_ctx + k].at[:, at], held.at[device_rows(k), at]))
        return [pltpu.make_async_copy(src, dst, arrived.at[late, i]) for i, (src, dst) in enumerate(copies)]

    def departures(j):
        columns = pl.ds(pl.multiple_of(j * width, HEAD_DIM), width)
        copies = [(dq_all.at[:, columns], dq_hbm.at[:, columns])]
        columns = pl.ds(pl.multiple_of(j * wide, HEAD_DIM), wide)
        first = 0
        for out in out_hbm:
            copies.append((staged.at[j, pl.ds(first, out.shape[0]), :], out.at[:, columns]))
            first += out.shape[0]
        return [pltpu.make_async_copy(src, dst, left.at[j, i]) for i, (src, dst) in enumerate(copies)]

    waves = [0] if calls == 1 else [0, 1]
    for late in waves:
        for copy in arrivals(late):
            copy.start()
    acc[...] = jnp.zeros_like(acc)
    for ref in operand:
        ref[...] = jnp.zeros_like(ref)
    offset = lax.broadcasted_iota(jnp.int32, (BLOCK, lanes), 0) - (
        lax.broadcasted_iota(jnp.int32, (BLOCK, lanes), 1) % BLOCK
    )

    def picks_of(j, b):
        own = me * blocks + b
        listed = [chosen[b, j, i] for i in range(topk)]
        return own, [own] + [jnp.where(listed[i] == own, listed[0], listed[i]) for i in range(1, topk)]

    def tile(i):
        return slice(i * BLOCK, (i + 1) * BLOCK)

    def block_rows(i):
        return pl.ds(pl.multiple_of(i * BLOCK, BLOCK), BLOCK)

    def columns_of(i):
        return pl.ds(pl.multiple_of(i * HEAD_DIM, HEAD_DIM), HEAD_DIM)

    def score_stage(j, b):
        _, picks = picks_of(j, b)
        for i in range(topk):
            near[b][tile(i), :HEAD_DIM] = k_all[block_rows(picks[i]), columns_of(j)]
            near[b][tile(i), HEAD_DIM:] = v_all[block_rows(picks[i]), columns_of(j)]
        for h in range(heads_per):
            at = columns_of(j * heads_per + h)
            operand[b][tile(h), :HEAD_DIM] = q_all[tile(b), at]
            operand[b][lanes + h * BLOCK : lanes + (h + 1) * BLOCK, HEAD_DIM:] = g_all[tile(b), at]
        scores[b][...] = lax.dot_general(
            near[b][...], operand[b][...], (((1,), (1,)), ((), ())), preferred_element_type=jnp.float32
        )

    def weight_stage(j, b):
        own, picks = picks_of(j, b)
        bias = [jnp.where(picks[i] > own, -1e30, 0.0) for i in range(topk)]
        score, weigh, pack = scores[b], scores[b], packed[b]
        first = jnp.where(offset <= 0, score[tile(0), :lanes], -1e30)
        top = first
        for i in range(1, topk):
            top = jnp.maximum(top, score[tile(i), :lanes] + bias[i])
        top = jnp.max(top, axis=0, keepdims=True)
        total = jnp.zeros((BLOCK, lanes), jnp.float32)
        delta = jnp.zeros((BLOCK, lanes), jnp.float32)
        for i in range(topk):
            s = first - top if i == 0 else score[tile(i), :lanes] - (top - bias[i])
            e = jnp.exp2(s * step)
            weigh[tile(i), :lanes] = e
            total = total + e
            delta = delta + e * score[tile(i), lanes:]
        total = 1.0 / jnp.sum(total, axis=0, keepdims=True)
        delta = jnp.sum(delta, axis=0, keepdims=True) * total
        for i in range(topk):
            w = weigh[tile(i), :lanes] * total
            pack[tile(i), lanes:] = w.astype(jnp.bfloat16)
            pack[tile(i), :lanes] = (w * (score[tile(i), lanes:] - delta)).astype(jnp.bfloat16)

    def term_stage(j, b):
        _, picks = picks_of(j, b)
        terms = jnp.dot(packed[b][...], operand[b][...], preferred_element_type=jnp.float32)
        for i in range(topk):
            acc[j, block_rows(picks[i]), :] += terms[tile(i), :]
        dq = scaling * lax.dot_general(
            near[b][:, :HEAD_DIM],
            packed[b][:, :lanes],
            (((0,), (0,)), ((), ())),
            preferred_element_type=jnp.float32,
        )
        dq = dq.T.astype(jnp.bfloat16)
        for h in range(heads_per):
            dq_all[tile(b), columns_of(j * heads_per + h)] = dq[tile(h), :]

    def leave(j):
        first = 0
        for cut in cuts:
            count = cut.stop - cut.start
            for core in range(2):
                for k in range(n_ctx // 2):
                    at = device_rows(2 * k + core, cut.start, count)
                    to = slice(first, first + count)
                    staged[j, to, :HEAD_DIM] = (acc[j, at, :HEAD_DIM] * scaling).astype(jnp.bfloat16)
                    staged[j, to, HEAD_DIM:] = acc[j, at, HEAD_DIM:].astype(jnp.bfloat16)
                    first += count
        for copy in departures(j):
            copy.start()

    def run(group, b, scoring=True, weighing=True, summing=True):
        if scoring:
            score_stage(group + b // blocks, b % blocks)
        if weighing:
            weight_stage(group + (b - 1) // blocks, (b - 1) % blocks)
        if summing:
            term_stage(group + (b - 2) // blocks, (b - 2) % blocks)

    def one_group(group, carry):
        for b in range(2, blocks + 2):
            run(group, b)
        leave(group)
        return carry

    for copy in arrivals(0):
        copy.wait()
    run(0, 0, weighing=False, summing=False)
    run(0, 1, summing=False)
    for late in waves[1:]:
        for copy in arrivals(late):
            copy.wait()
    lax.fori_loop(0, calls - 1, one_group, 0)
    for b in range(2, blocks):
        run(calls - 1, b)
    run(calls - 1, blocks, scoring=False)
    run(calls - 1, blocks + 1, scoring=False, weighing=False)
    leave(calls - 1)
    for j in range(calls):
        for copy in departures(j):
            copy.wait()


def attention(axis, pieces, queries, grad_out, chosen, cuts):
    n_ctx = len(pieces) // 2
    rows = queries.shape[0]
    topk = chosen.shape[-1]
    wide = 2 * HEAD_DIM
    groups = pieces[0].shape[1] // HEAD_DIM
    width = queries.shape[1] // groups
    lanes = width // HEAD_DIM * BLOCK
    blocks = rows // BLOCK
    near = topk * BLOCK
    flops = groups * blocks * 10 * near * lanes * HEAD_DIM
    sizes = [n_ctx // 2 * (cut.stop - cut.start) for cut in cuts for core in range(2)]
    bf16 = lambda *shape: pltpu.VMEM(shape, jnp.bfloat16)
    f32 = lambda *shape: pltpu.VMEM(shape, jnp.float32)
    anywhere = pl.BlockSpec(memory_space=pl.ANY)
    return pl.pallas_call(
        functools.partial(attention_kernel, axis, n_ctx, topk, cuts),
        out_shape=[jax.ShapeDtypeStruct(queries.shape, jnp.bfloat16)]
        + [jax.ShapeDtypeStruct((size, groups * wide), jnp.bfloat16) for size in sizes],
        in_specs=[anywhere] * (2 * n_ctx + 3),
        out_specs=[anywhere] * (1 + len(sizes)),
        scratch_shapes=[
            bf16(n_ctx * rows, groups * HEAD_DIM),
            bf16(n_ctx * rows, groups * HEAD_DIM),
            bf16(*queries.shape),
            bf16(*queries.shape),
            f32(groups, n_ctx * rows, wide),
            [bf16(near, wide)] * blocks,
            [f32(near, 2 * lanes)] * blocks,
            [bf16(near, 2 * lanes)] * blocks,
            [bf16(2 * lanes, wide)] * blocks,
            bf16(*queries.shape),
            bf16(groups, n_ctx * rows, wide),
            pltpu.SMEM(chosen.shape, jnp.int32),
            pltpu.SemaphoreType.DMA((2, 2 * n_ctx + 3)),
            pltpu.SemaphoreType.DMA((groups, 1 + len(sizes))),
        ],
        compiler_params=pltpu.CompilerParams(vmem_limit_bytes=28 * 2**20),
        cost_estimate=pl.CostEstimate(flops=flops, bytes_accessed=16 * n_ctx * rows * wide * groups, transcendentals=0),
        name="attention",
    )(in_hbm(chosen), *pieces, in_hbm(queries), in_hbm(grad_out))


def query_term_kernel(gq_ref, w_ref, out_ref):
    out_ref[...] = lax.dot_general(
        gq_ref[...], w_ref[...], (((1,), (1,)), ((), ())), preferred_element_type=jnp.float32
    ).astype(jnp.bfloat16)


def query_term(shares, gq, w):
    rows, depth = gq.shape
    width = w.shape[0] // shares
    return pl.pallas_call(
        query_term_kernel,
        out_shape=jax.ShapeDtypeStruct((shares, rows, width), jnp.bfloat16),
        grid=(shares,),
        in_specs=[pl.BlockSpec((rows, depth), lambda j: (0, 0)), pl.BlockSpec((width, depth), lambda j: (j, 0))],
        out_specs=pl.BlockSpec((None, rows, width), lambda j: (j, 0, 0)),
        compiler_params=pltpu.CompilerParams(vmem_limit_bytes=16 * 2**20),
        cost_estimate=pl.CostEstimate(
            flops=2 * shares * width * rows * depth, bytes_accessed=2 * shares * width * depth, transcendentals=0
        ),
        name="query_term",
    )(gq, w)


def projection_kernel(axis, places, cut, summed, *refs):
    count = len(places)
    parts, (term, wk_hbm, wv_hbm), refs = refs[:summed], refs[summed : summed + 3], refs[summed + 3 :]
    if summed > 2:
        gk_hbm, gv_hbm, *refs = refs
    out_hbm, (wk, wv, terms, held, gk, gv, out, w_sem, part_sem, out_sem) = refs[:count], refs[count:]
    width = wk.shape[1]
    rows = cut.stop - cut.start
    n = lax.axis_size(axis)
    order = [line_order(n, lax.axis_index(axis))[i] for i in places]

    def arrivals(i):
        at = pl.ds(pl.multiple_of(order[i] * width, width), width)
        copies = ((wk_hbm.at[at, :], wk), (wv_hbm.at[at, :], wv), (term.at[order[i], pl.ds(cut.start, rows), :], terms))
        return [pltpu.make_async_copy(src, dst.at[i], w_sem.at[i, k]) for k, (src, dst) in enumerate(copies)]

    targets = [held.at[i] for i in range(summed)] if summed > 2 else [gk, gv]
    part_copies = [
        pltpu.make_async_copy(src.at[pl.ds(0, rows), :], dst, part_sem.at[i])
        for i, (src, dst) in enumerate(zip(parts, targets))
    ]
    for copy in part_copies:
        copy.start()
    for i in range(count):
        for copy in arrivals(i):
            copy.start()
    for copy in part_copies:
        copy.wait()
    leaving = []

    def leave(src, dst):
        leaving.append(pltpu.make_async_copy(src, dst, out_sem.at[len(leaving)]))
        leaving[-1].start()

    if summed > 2:
        for g in range(gk.shape[1] // HEAD_DIM):
            for side, total_ref in ((0, gk), (1, gv)):
                at = slice((2 * g + side) * HEAD_DIM, (2 * g + side + 1) * HEAD_DIM)
                total = held[0, :, at].astype(jnp.float32)
                for i in range(1, summed):
                    total += held[i, :, at].astype(jnp.float32)
                total_ref[:, g * HEAD_DIM : (g + 1) * HEAD_DIM] = total.astype(jnp.bfloat16)
        leave(gk, gk_hbm)
        leave(gv, gv_hbm)
    contract = (((1,), (1,)), ((), ()))
    for i in range(count):
        for copy in arrivals(i):
            copy.wait()
        total = terms[i].astype(jnp.float32)
        total += lax.dot_general(gk[...], wk[i], contract, preferred_element_type=jnp.float32)
        total += lax.dot_general(gv[...], wv[i], contract, preferred_element_type=jnp.float32)
        out[i] = total.astype(jnp.bfloat16)
        leave(out.at[i], out_hbm[i])
    for copy in leaving:
        copy.wait()


def projection(axis, places, cut, parts, term, weights):
    count = len(places)
    summed = len(parts)
    rows = cut.stop - cut.start
    columns = weights[0].shape[1]
    width = term.shape[2]
    out_shape = [pltpu.HBM((rows, width), jnp.bfloat16)] * count
    if summed > 2:
        out_shape = [jax.ShapeDtypeStruct((rows, columns), jnp.bfloat16)] * 2 + out_shape
    bf16 = lambda *shape: pltpu.VMEM(shape, jnp.bfloat16)
    anywhere = pl.BlockSpec(memory_space=pl.ANY)
    return pl.pallas_call(
        functools.partial(projection_kernel, axis, places, cut, summed),
        out_shape=out_shape,
        in_specs=[anywhere] * (summed + 3),
        out_specs=[anywhere] * len(out_shape),
        scratch_shapes=[
            bf16(count, width, columns),
            bf16(count, width, columns),
            bf16(count, rows, width),
            bf16(summed, rows, parts[0].shape[1]),
            bf16(rows, columns),
            bf16(rows, columns),
            bf16(count, rows, width),
            pltpu.SemaphoreType.DMA((count, 3)),
            pltpu.SemaphoreType.DMA((summed,)),
            pltpu.SemaphoreType.DMA((len(out_shape),)),
        ],
        compiler_params=pltpu.CompilerParams(vmem_limit_bytes=16 * 2**20),
        cost_estimate=pl.CostEstimate(
            flops=4 * count * width * rows * columns, bytes_accessed=4 * count * width * columns, transcendentals=0
        ),
        name="projection",
    )(*parts, term, *map(in_hbm, weights))


def exchange(x, axis, mask):
    n = lax.axis_size(axis)
    return lax.ppermute(x, axis, [(i, i ^ mask) for i in range(n)])


def gather_pieces(sides, axis):
    n = lax.axis_size(axis)
    pieces = [{0: side} for side in sides]
    for mask in sorted(range(2, n, 2), key=lambda m: (m.bit_count(), m)):
        bits = [1 << i for i in range(n.bit_length()) if mask >> i & 1]
        for i, held in enumerate(pieces):
            bit = bits[(i - 1) % len(bits)]
            held[mask] = exchange(held[mask ^ bit], axis, bit)
    for held in pieces:
        for mask in range(0, n, 2):
            held[mask | 1] = exchange(held[mask], axis, 1)
    return [held[k] for held in pieces for k in range(n)]


def scatter_parts(keep, got, axis):
    n = lax.axis_size(axis)
    rows = keep.shape[0] // (n // 2)
    sums = {}
    for mask in range(n - 2, 0, -2):
        cut = slice(mask // 2 * rows, (mask // 2 + 1) * rows)
        sums[mask] = (keep[cut].astype(jnp.float32) + got[cut].astype(jnp.float32)).astype(jnp.bfloat16)
    return [keep, got] + [exchange(x, axis, mask) for mask, x in sums.items()], list(sums.values())


def line_order(n, me):
    if n == 4:
        return [me ^ 2, me ^ 3, me ^ 1, me]
    return [(me + 1 + i) % n for i in range(n)]


def line_sum(chunks, axis, after):
    n = lax.axis_size(axis)
    me = lax.axis_index(axis)
    wide = lambda x: x.astype(jnp.float32)
    if after:
        chunks[1:], _ = lax.optimization_barrier((chunks[1:], after))
    if n == 4:
        first, second, third, own = chunks
        got_first = lax.ppermute(first, axis, [(0, 1), (3, 2), (1, 3), (2, 0)])
        got_second = lax.ppermute(second, axis, [(0, 3), (3, 0)])
        got_third = lax.ppermute(third, axis, [(0, 1), (2, 3), (1, 0), (3, 2)])
        passed = (wide(second) + wide(got_first)).astype(jnp.bfloat16)
        got_passed = lax.ppermute(passed, axis, [(1, 2), (2, 1)])
        outer = jnp.logical_or(me == 0, me == 3)
        total = wide(own) + jnp.where(outer, wide(got_first), 0.0)
        return (total + wide(got_second) + wide(got_third) + wide(got_passed)).astype(jnp.bfloat16), [
            got_first,
            got_second,
            got_third,
        ]
    stacked = jnp.stack(chunks)

    def chunk(d):
        return wide(lax.dynamic_index_in_dim(stacked, (d - me - 1) % n, 0, keepdims=False))

    from_left = from_right = 0.0
    for t in range(1, n):
        right = (chunk(n - t + me) + from_left).astype(jnp.bfloat16)
        left = (chunk(t - n + me) + from_right).astype(jnp.bfloat16)
        from_left = wide(lax.ppermute(right, axis, [(i, i + 1) for i in range(t)]))
        from_right = wide(lax.ppermute(left, axis, [(n - 1 - i, n - 2 - i) for i in range(t)]))
    return (chunk(me) + from_left + from_right).astype(jnp.bfloat16), [from_left, from_right]


def body(queries, keys, values, grad_out, chosen, w_query, w_key, w_value):
    rows = queries.shape[0]
    front = rows * 5 // 16 // 16 * 16
    cuts = [slice(0, front), slice(front, rows)]
    shares = lax.axis_size("head")
    pieces = gather_pieces((keys, values), "ctx")
    pieces[0], pieces[len(pieces) // 2] = in_hbm(keys), in_hbm(values)
    grad_queries, *terms = attention("ctx", pieces, queries, grad_out, chosen, cuts)
    held = []
    for keep, send in zip(terms[::2], terms[1::2]):
        if held:
            send, _ = lax.optimization_barrier((send, held[-1][1]))
        held.append((keep, exchange(send, "ctx", 1)))
    term = query_term(shares, grad_queries, w_query)
    weights = (w_key, w_value)
    received = []
    sent = []
    for keep, got in held:
        if sent:
            keep, got, _ = lax.optimization_barrier((keep, got, sent))
        arrived, sent = scatter_parts(keep, got, "ctx")
        received.append(arrived)
    grads = []
    after = []
    for cut, arrived in zip(cuts, received):
        early = shares // 2 if after else shares - 1
        grad_k, grad_v, *chunks = projection("head", range(early), cut, arrived, term, weights)
        chunks += projection("head", range(early, shares), cut, [grad_k, grad_v], term, weights)
        total, after = line_sum(chunks, "head", after)
        grads.append((grad_k, grad_v, total))
    grad_keys, grad_values, grad_input = (
        lax.dynamic_update_slice(jnp.pad(head, ((0, tail.shape[0]), (0, 0))), tail, (head.shape[0], 0))
        for head, tail in zip(*grads)
    )
    return (grad_queries, grad_keys, grad_values, grad_input)


def solution(mesh):
    return jax.shard_map(
        body,
        mesh=mesh,
        in_specs=(
            P("ctx", "head"),
            P("ctx", "head"),
            P("ctx", "head"),
            P("ctx", "head"),
            P("ctx", "head", None),
            P(None, "head"),
            P(None, "head"),
            P(None, "head"),
        ),
        out_specs=(P("ctx", "head"), P("ctx", "head"), P("ctx", "head"), P("ctx", "head")),
        check_vma=False,
    )
```
